32 devices in a mesh: cfg: 2 (over core), seq: 4 (over y, x), tp: 4 (over z).
Axes of the slice: x: 2, y: 2, z: 4, core: 2. Of those that a mesh axis runs over, the one named last changes fastest.
Arguments:
- stream: bfloat16 [2, 160, 3072], P('cfg', 'seq', 'tp'), may hold values from -6 to 6
- queries: bfloat16 [2, 160, 1536], P('cfg', 'seq', 'tp'), may hold values from -6 to 6
- keys: bfloat16 [2, 160, 1536], P('cfg', 'seq', 'tp'), may hold values from -6 to 6
- values: bfloat16 [2, 160, 1536], P('cfg', 'seq', 'tp'), may hold values from -6 to 6
- text_keys: bfloat16 [2, 226, 1536], P('cfg', None, 'tp'), may hold values from -6 to 6
- text_values: bfloat16 [2, 226, 1536], P('cfg', None, 'tp'), may hold values from -6 to 6
- out_weight: bfloat16 [1536, 3072], P('tp'), may hold values from -0.15625 to 0.15625
- gate: float32 [3072], P('tp'), may hold values from -4 to 4
- shift: float32 [3072], P('tp'), may hold values from -3 to 3
- scale: float32 [3072], P('tp'), may hold values from -3 to 3
- proj_weight: float32 [3072, 64], P('tp'), may hold values from -0.109375 to 0.109375
- q_gain: float32 [64], replicated, may hold values from 1.4 to 6
- k_gain: float32 [64], replicated, may hold values from 1.4 to 6
- lengths: int32 [4], replicated, may hold values from 1 to 40, 144 in all
- latents: float32 [160, 64], P('seq', ('cfg', 'tp')), may hold values from -6 to 6
- alphas: float32 [1000], replicated, may hold values from 0.05 to 0.95
- step_index: int32 [1], replicated, may hold values from 20 to 999
Outputs:
- hidden_out: bfloat16 [2, 160, 3072], P('cfg', 'seq', 'tp')
- latents_out: float32 [160, 64], P('seq', ('cfg', 'tp'))
The draws below stay inside these ranges and needn't reach their ends.
Inputs may be any that keep to these rules, and one draw needn't show every extreme that they name: `lengths`: video tokens held by each index of seq, in token order; they sum to 144 and the largest is exactly 40. The previous step's entry is step_index - 20.
All inputs are finite; a program needn't handle non-finite values.
Results may differ from the reference program's by a relative error of at most 0.012.
The reference program's roundings to bfloat16 on the way (of `query_hat`, `key_hat`, `rounded` and `attended`) count: a program that leaves them out, or rounds other values in their place, can miss the bound.
Values may be sent and summed in bfloat16 or wider, within the bound.
No kernel may reach another device: no remote copies, remote signals or barrier semaphores. Data moves between devices by JAX's collectives and lax.ppermute only.
A program may use at most 64 MiB of HBM per device.

```python
import math
import jax
import jax.numpy as jnp
import numpy as np
from jax import lax

D = 3072
HEADS = 24
HEAD = 64
TXT = 226
HP = 30
WP = 45
CHAN = 64
CAP = 40
TABLE = 1000
STRIDE = 20
HALVES = 2
ROWS = 160
VID = 144
N_SEQ = 4


def shared_rows(key):
    shape = (HALVES, ROWS, HEADS * HEAD)
    first = jax.random.normal(jax.random.fold_in(key, 11), shape, jnp.float32)
    second = jax.random.normal(jax.random.fold_in(key, 12), shape, jnp.float32)
    return (first, second)


def draw_queries(key, part):
    first, second = shared_rows(key)
    return jnp.clip(first, -6.0, 6.0).astype(jnp.bfloat16)


def draw_keys(key, part):
    first, second = shared_rows(key)
    return jnp.clip(second, -6.0, 6.0).astype(jnp.bfloat16)


def draw_q_gain(key, part):
    inner = jax.random.fold_in(key, 21)
    return jax.random.uniform(inner, (HEAD,), jnp.float32, 1.4, 2.4)


def draw_k_gain(key, part):
    inner = jax.random.fold_in(key, 22)
    return jax.random.uniform(inner, (HEAD,), jnp.float32, 1.4, 2.4)


def level_of(own_key, dims, cuts, low, top_value):
    def one(dim, parts):
        steps = jax.random.uniform(jax.random.fold_in(jax.random.fold_in(own_key, 6), dim), (parts,), jnp.float32, low / len(cuts), top_value / len(cuts))
        return jnp.repeat(jnp.exp(steps), dims[dim] // parts).reshape((-1,) + (1,) * (len(dims) - dim - 1))

    loudness = one(*cuts[0])
    for cut in cuts[1:]:
        loudness = loudness * one(*cut)
    return loudness


def profile(number_of, total, bound, skew):
    portions = [(1 << 20) // math.isqrt(standing ** skew) + 1 for standing in range(2, number_of + 1)]
    rest, holding = total - bound - (number_of - 1), [1] * (number_of - 1)
    while rest > 0:
        movable = [i for i in range(number_of - 1) if holding[i] < bound]
        mass, remaining = sum([portions[i] for i in movable]), rest
        for i in movable:
            extra = min(bound - holding[i], max(1, remaining * portions[i] // mass), rest)
            holding[i] = holding[i] + extra
            rest = rest - extra
    return np.array([bound] + holding)


def ragged_sizes(stream_key, count, total, limit, slope):
    if count == 2:
        one = jax.random.randint(stream_key, (), max(1, total - limit), min(limit, total - 1) + 1)
        return jnp.stack([one, total - one])
    sizes = jnp.asarray(profile(count, total, limit, slope), jnp.int32)
    couples = (count - 1) // 2
    source_of, taker = sizes[1:1 + 2 * couples:2], sizes[2:2 + 2 * couples:2]
    slack = jnp.minimum(source_of - 1, limit - taker)
    passed = jax.random.randint(jax.random.fold_in(stream_key, 1), (couples,), 0, 1 << 20) % (slack + 1)
    sizes = sizes.at[1:1 + 2 * couples:2].set(source_of - passed).at[2:2 + 2 * couples:2].set(taker + passed)
    return sizes[jax.random.permutation(jax.random.fold_in(stream_key, 2), count)]


def scatter_about(stream_key, shape, scale, reach, shards=(), held_as=jnp.bfloat16):
    entries = scale * jax.random.normal(stream_key, shape, jnp.float32)
    if shards:
        entries = entries * level_of(stream_key, shape, shards, -0.22, 0.18)
    return jnp.clip(entries, -reach, reach).astype(held_as)


def setup_inputs(seed: int = 0) -> dict:
    key_of = jax.random.split(jax.random.key(seed), 18)
    stream = scatter_about(key_of[0], (HALVES, ROWS, D), 1.0, 6.0, ((0, 2), (1, 4), (2, 4)))
    queries = draw_queries(jax.random.fold_in(key_of[17], 71), 0)
    keys = draw_keys(jax.random.fold_in(key_of[17], 71), 0)
    values = scatter_about(key_of[3], (HALVES, ROWS, HEADS * HEAD), 1.0, 6.0, ((0, 2), (1, 4), (2, 4)))
    text_keys = scatter_about(key_of[4], (HALVES, TXT, HEADS * HEAD), 1.0, 6.0, ((0, 2), (2, 4)))
    text_values = scatter_about(key_of[5], (HALVES, TXT, HEADS * HEAD), 1.0, 6.0, ((0, 2), (2, 4)))
    out_weight = scatter_about(key_of[6], (HEADS * HEAD, D), (HEADS * HEAD) ** -0.5, 0.15625, ((0, 4),))
    gate = scatter_about(key_of[7], (D,), 1.0, 4.0, ((0, 4),), jnp.float32)
    shift = scatter_about(key_of[8], (D,), 0.5, 3.0, ((0, 4),), jnp.float32)
    scale = scatter_about(key_of[9], (D,), 0.5, 3.0, ((0, 4),), jnp.float32)
    proj_weight = scatter_about(key_of[10], (D, CHAN), D ** -0.5, 0.109375, ((0, 4),), jnp.float32)
    q_gain = draw_q_gain(jax.random.fold_in(key_of[17], 71), 0)
    k_gain = draw_k_gain(jax.random.fold_in(key_of[17], 71), 0)
    lengths = ragged_sizes(key_of[13], N_SEQ, VID, CAP, 2).astype(jnp.int32)
    latents = scatter_about(key_of[14], (ROWS, CHAN), 1.0, 6.0, ((0, 4), (1, 8)), jnp.float32)
    alphas = jnp.clip(jax.random.uniform(key_of[15], (TABLE,), jnp.float32, 0.05, 0.95), 0.05, 0.95)
    step_index = jax.random.randint(key_of[16], (1,), STRIDE, TABLE).astype(jnp.int32)
    return {"stream": stream, "queries": queries, "keys": keys, "values": values, "text_keys": text_keys, "text_values": text_values, "out_weight": out_weight, "gate": gate, "shift": shift, "scale": scale, "proj_weight": proj_weight, "q_gain": q_gain, "k_gain": k_gain, "lengths": lengths, "latents": latents, "alphas": alphas, "step_index": step_index}


guide_scale = 6.0
head_eps = 1e-06
final_eps = 1e-05

def rope_tables(position):
    frame = position // (HP * WP)
    height = position // WP % HP
    across = position % WP

    def angles(coord, extent):
        freq = 1.0 / 10000.0 ** (jnp.arange(0, extent, 2, dtype=jnp.float32) / extent)
        return coord.astype(jnp.float32)[:, None] * freq[None, :]
    angle = jnp.concatenate([angles(frame, 16), angles(height, 24), angles(across, 24)], axis=1)
    return (jnp.cos(angle), jnp.sin(angle))

def head_norm(field, gain):
    centre = field - lax.optimization_barrier(jnp.mean(field, axis=-1, keepdims=True))
    spread = lax.optimization_barrier(jnp.mean(centre * centre, axis=-1, keepdims=True))
    return centre * lax.rsqrt(spread + head_eps) * gain

def rotate_pairs(field, cos_table, sin_table):
    pairs = field.reshape(field.shape[:-1] + (HEAD // 2, 2))
    first = pairs[..., 0]
    second = pairs[..., 1]
    cos_part = cos_table[:, None, :]
    sin_part = sin_table[:, None, :]
    turned = jnp.stack([first * cos_part - second * sin_part, second * cos_part + first * sin_part], axis=-1)
    return turned.reshape(field.shape)

def prepare(field, gain, tables):
    count = field.shape[0]
    normed = head_norm(field.astype(jnp.float32).reshape(count, -1, HEAD), gain)
    if tables is not None:
        normed = rotate_pairs(normed, tables[0], tables[1])
    return normed.reshape(count, -1).astype(jnp.bfloat16)

def reference(stream, queries, keys, values, text_keys, text_values, out_weight, gate, shift, scale, proj_weight, q_gain, k_gain, lengths, latents, alphas, step_index):
    offsets = jnp.cumsum(lengths) - lengths
    slots = jnp.arange(ROWS, dtype=jnp.int32)
    owner = (slots // CAP).astype(jnp.int32)
    within = (slots % CAP).astype(jnp.int32)
    position = (offsets[owner] + within).astype(jnp.int32)
    live = within < lengths[owner]
    tables = rope_tables(position)
    key_live = jnp.concatenate([jnp.arange(TXT, dtype=jnp.int32) >= 0, live])
    predictions = []
    hiddens = []
    for half in range(HALVES):
        query_hat = lax.optimization_barrier(prepare(queries[half], q_gain, tables))
        query_hat = query_hat.astype(jnp.float32).reshape(N_SEQ, CAP, HEADS, HEAD)
        key_hat = jnp.concatenate([prepare(text_keys[half], k_gain, None), prepare(keys[half], k_gain, tables)], axis=0)
        key_hat = lax.optimization_barrier(key_hat).astype(jnp.float32).reshape(-1, HEADS, HEAD)
        value_all = jnp.concatenate([text_values[half], values[half]], axis=0).astype(jnp.float32).reshape(-1, HEADS, HEAD)

        def attend(block):
            scores = jnp.einsum('qhd,khd->hqk', block, key_hat) * 0.125
            scores = jnp.where(key_live[None, None, :], scores, -jnp.inf)
            row_max = lax.optimization_barrier(jnp.max(scores, axis=-1, keepdims=True))
            weights = jnp.exp(scores - row_max)
            totals = lax.optimization_barrier(jnp.sum(weights, axis=-1))
            rounded = lax.optimization_barrier(weights.astype(jnp.bfloat16)).astype(jnp.float32)
            mixed = jnp.einsum('hqk,khd->qhd', rounded, value_all) / jnp.transpose(totals)[:, :, None]
            return mixed.astype(jnp.bfloat16).reshape(CAP, HEADS * HEAD)
        attended = lax.map(attend, query_hat).reshape(ROWS, HEADS * HEAD)
        projected = jnp.dot(attended, out_weight, preferred_element_type=jnp.float32)
        hidden = stream[half].astype(jnp.float32) + gate * projected
        hidden = jnp.where(live[:, None], hidden, 0.0).astype(jnp.bfloat16)
        hiddens.append(hidden)
        widened = lax.optimization_barrier(hidden).astype(jnp.float32)
        mean = lax.optimization_barrier(jnp.sum(widened, axis=1, keepdims=True)) / D
        square = lax.optimization_barrier(jnp.sum(widened * widened, axis=1, keepdims=True)) / D
        normed = (widened - mean) * lax.rsqrt(square - mean * mean + final_eps) * (1.0 + scale) + shift
        predictions.append(jnp.dot(normed, proj_weight, precision=lax.Precision.HIGHEST, preferred_element_type=jnp.float32))
    guided = predictions[1] + guide_scale * (predictions[0] - predictions[1])
    current = alphas[step_index[0]]
    earlier = alphas[step_index[0] - STRIDE]
    root_now = jnp.sqrt(current)
    rest_now = jnp.sqrt(1.0 - current)
    clean = root_now * latents - rest_now * guided
    noise = root_now * guided + rest_now * latents
    stepped = jnp.sqrt(earlier) * clean + jnp.sqrt(1.0 - earlier) * noise
    latents_out = jnp.where(live[:, None], stepped, 0.0)
    return (jnp.stack(hiddens), latents_out)
```

```python
import functools
import math

import jax
import jax.numpy as jnp
from jax import lax
from jax.experimental import pallas as pl
from jax.experimental.pallas import tpu as pltpu
from jax.sharding import PartitionSpec as P

HEAD = 64
PAIR = 2 * HEAD
HP = 30
WP = 45
STRIDE = 20
LANES = 128

guide_scale = 6.0
head_eps = 1e-06
final_eps = 1e-05

F32 = jnp.float32
BF16 = jnp.bfloat16
VMEM_LIMIT = 24 * 1024 * 1024


def call(kernel, outs, n_in, smem=(), hbm=(), scratch=(), cost=0):
    spaces = [
        pltpu.SMEM if i in smem else pl.ANY if i in hbm else pltpu.VMEM for i in range(n_in)
    ]
    many = isinstance(outs, (list, tuple))
    vmem = pl.BlockSpec(memory_space=pltpu.VMEM)
    return pl.pallas_call(
        kernel,
        out_shape=outs,
        in_specs=[pl.BlockSpec(memory_space=s) for s in spaces],
        out_specs=[vmem] * len(outs) if many else vmem,
        scratch_shapes=list(scratch),
        compiler_params=pltpu.CompilerParams(vmem_limit_bytes=VMEM_LIMIT),
        cost_estimate=pl.CostEstimate(flops=cost, bytes_accessed=cost // 64, transcendentals=0),
    )


def shape(dims, dtype=F32):
    return jax.ShapeDtypeStruct(dims, dtype)


def rows_of(parts, dtype):
    return jnp.concatenate([p.astype(F32) for p in parts], axis=0).astype(dtype)


def nt(left, right):
    return lax.dot_general(left, right, (((1,), (1,)), ((), ())), preferred_element_type=F32)


def nn(left, right):
    return jnp.dot(left, right, preferred_element_type=F32)


def prior(lengths, rank, blocks):
    total = jnp.int32(0)
    for i in range(blocks):
        total = total + jnp.where(i < rank, lengths[i], 0)
    return total


def averager():
    row = lax.broadcasted_iota(jnp.int32, (PAIR, PAIR), 0)
    col = lax.broadcasted_iota(jnp.int32, (PAIR, PAIR), 1)
    return jnp.where((row < HEAD) == (col < HEAD), 1.0 / HEAD, 0.0).astype(BF16)


def head_norm(field, average, gain):
    centre = field.astype(F32) - nn(field, average)
    square = centre * centre
    high = square.astype(BF16)
    low = (square - high.astype(F32)).astype(BF16)
    spread = nn(high, average) + nn(low, average)
    return centre * lax.rsqrt(spread + head_eps) * gain


def rope_tables(start, rows):
    lane = lax.broadcasted_iota(jnp.int32, (rows, PAIR), 1)
    pos = (lax.broadcasted_iota(jnp.int32, (rows, PAIR), 0) + start).astype(F32)
    frame = jnp.floor((pos + 0.5) * (1.0 / (HP * WP)))
    line = jnp.floor((pos + 0.5) * (1.0 / WP))
    across = pos - line * WP
    height = line - frame * HP
    pair = (lane % HEAD) // 2
    in_frame = pair < 8
    in_height = pair < 20
    coord = jnp.where(in_frame, frame, jnp.where(in_height, height, across))
    step = jnp.where(in_frame, pair, jnp.where(in_height, pair - 8, pair - 20)).astype(F32)
    rate = jnp.where(in_frame, 2.0 / 16, 2.0 / 24)
    angle = coord * jnp.exp(step * rate * (-math.log(10000.0)))
    sine = jnp.sin(angle)
    return jnp.cos(angle), jnp.where(lane % 2 == 0, -sine, sine)


def rotate(field, cos_table, sin_table):
    even = lax.broadcasted_iota(jnp.int32, field.shape, 1) % 2 == 0
    other = jnp.where(even, pltpu.roll(field, PAIR - 1, 1), pltpu.roll(field, 1, 1))
    return field * cos_table + other * sin_table


def twice(gain_ref):
    gain = gain_ref[...]
    return jnp.concatenate([gain, gain], axis=1)


def pack_keys_kernel(blocks, lengths, keys, values, gain, packed):
    rows, width = keys.shape[1:]
    start = prior(lengths, lax.axis_index("seq"), blocks)
    tables = rope_tables(start, rows)
    average, gain = averager(), twice(gain)
    for at in range(0, width, PAIR):
        normed = head_norm(keys[0, :, at : at + PAIR], average, gain)
        packed[:, at : at + PAIR] = rotate(normed, *tables).astype(BF16)
    packed[:, width:] = values[0]


def queries_kernel(blocks, order, lengths, queries, text_keys, q_gain, k_gain, stacked, text_scores, bias):
    rows, width = queries.shape[1:]
    rank = lax.axis_index("seq")
    tables = rope_tables(prior(lengths, rank, blocks), rows)
    average, q_gain, k_gain = averager(), twice(q_gain), twice(k_gain)
    left = lax.broadcasted_iota(jnp.int32, (rows, PAIR), 1) < HEAD
    for p, at in enumerate(range(0, width, PAIR)):
        query = rotate(head_norm(queries[0, :, at : at + PAIR], average, q_gain), *tables)
        query = query.astype(BF16).astype(F32) * 0.125
        both = jnp.concatenate([jnp.where(left, query, 0.0), jnp.where(left, 0.0, query)], axis=0)
        both = both.astype(BF16)
        stacked[p] = both
        key = head_norm(text_keys[0, :, at : at + PAIR], average, k_gain).astype(BF16)
        text_scores[p] = nt(both, key)
    lane = lax.broadcasted_iota(jnp.int32, bias.shape, 1)
    live = lane < 0
    for i, block in enumerate(order(rank)):
        live = live | ((lane >= i * rows) & (lane < i * rows + lengths[block]))
    bias[...] = jnp.where(live, 0.0, -jnp.inf)


def attend_kernel(n_blocks, sends, stacked, text_scores, bias, text_values, weight, *rest):
    gathered = rest[:n_blocks]
    attended, outs = rest[n_blocks], rest[n_blocks + 1 : -2]
    held, sem = rest[-2:]
    fetch = pltpu.make_async_copy(weight, held, sem)
    fetch.start()
    pairs, double = stacked.shape[:2]
    rows, width = double // 2, pairs * PAIR
    if n_blocks > 1:
        video = rows_of([g[...] for g in gathered], BF16)
    else:
        video = gathered[0][...]
    left = lax.broadcasted_iota(jnp.int32, (rows, PAIR), 1) < HEAD
    parts = []
    for p in range(pairs):
        at = p * PAIR
        scores_t = text_scores[p]
        scores_v = nt(stacked[p], video[:, at : at + PAIR]) + bias[...]
        row_max = jnp.maximum(
            jnp.max(scores_t, axis=1, keepdims=True), jnp.max(scores_v, axis=1, keepdims=True)
        )
        weights_t = jnp.exp(scores_t - row_max)
        weights_v = jnp.exp(scores_v - row_max)
        totals = jnp.sum(weights_t, axis=1, keepdims=True) + jnp.sum(weights_v, axis=1, keepdims=True)
        mixed = nn(weights_t.astype(BF16), text_values[0, :, at : at + PAIR])
        mixed = mixed + nn(weights_v.astype(BF16), video[:, width + at : width + at + PAIR])
        mixed = mixed / totals
        parts.append(jnp.where(left, mixed[:rows], mixed[rows:]).astype(BF16))
    joined = jnp.concatenate(parts, axis=1)
    attended[...] = joined
    fetch.wait()
    rank = lax.axis_index("tp")
    for out, block in zip(outs, sends(rank)):
        columns = out.shape[1]
        out[...] = nn(joined, held[:, pl.ds(pl.multiple_of(block * columns, columns), columns)]).astype(BF16)


def residual_kernel(
    tp, lengths, alphas, step, attended, weight, stream, gate, shift, scale, proj, latents,
    base, factor, mask, split, consts, coefs, held, sem,
):
    rank = lax.axis_index("tp")
    rows, columns = base.shape
    fetch = pltpu.make_async_copy(
        weight.at[:, pl.ds(pl.multiple_of(rank * columns, columns), columns)], held, sem
    )
    fetch.start()
    count = lengths[lax.axis_index("seq")]
    row = lax.broadcasted_iota(jnp.int32, mask.shape, 0)
    mask[...] = jnp.where(row < count, 1.0, 0.0)
    factor[...] = jnp.where(row[:, :1] < count, gate[...], 0.0)
    channels = proj.shape[0]
    plain = proj[...]
    scaled = plain * (1.0 + scale[...])
    high = scaled.astype(BF16)
    rest = scaled - high.astype(F32)
    middle = rest.astype(BF16)
    split[0:channels] = high
    split[channels : 2 * channels] = middle
    split[2 * channels : 3 * channels] = (rest - middle.astype(F32)).astype(BF16)
    split[3 * channels :] = jnp.ones((16, columns), BF16)
    lane = lax.broadcasted_iota(jnp.int32, consts.shape, 1)
    consts[...] = jnp.where(
        lane == rows,
        jnp.sum(scaled, axis=1, keepdims=True),
        jnp.where(lane == rows + 1, jnp.sum(plain * shift[...], axis=1, keepdims=True), 0.0),
    )
    at = step[0]
    now = jnp.full((8, LANES), alphas[at], F32)
    earlier = jnp.full((8, LANES), alphas[at - STRIDE], F32)
    coefs[0:8] = jnp.sqrt(now)
    coefs[8:16] = jnp.sqrt(1.0 - now)
    coefs[16:24] = jnp.sqrt(earlier)
    coefs[24:32] = jnp.sqrt(1.0 - earlier)
    lane8 = lax.broadcasted_iota(jnp.int32, (8, LANES), 1)
    coefs[32:40] = jnp.where(lane8 < count, 1.0, 0.0)
    coefs[40:48] = jnp.concatenate([latents[...], jnp.zeros((8, LANES - rows), F32)], axis=1)
    fetch.wait()
    base[...] = jnp.where(
        row[:, :1] < count, stream[0].astype(F32) + gate[...] * nn(attended[...], held[...]), 0.0
    )


def hidden_kernel(tp, base, factor, mask, split, consts, *rest):
    arrived, (hidden, *outs), scratch = rest[: tp - 1], rest[tp - 1 : -1], rest[-1]
    summed = arrived[0][...].astype(F32)
    for block in arrived[1:]:
        summed = summed + block[...].astype(F32)
    value = (base[...] + factor[...] * summed).astype(BF16)
    hidden[0] = value
    rows = value.shape[0]
    channels = consts.shape[0]
    wide = value.astype(F32)
    square = wide * wide
    high = square.astype(BF16)
    low = (square - high.astype(F32)).astype(BF16)
    ones = split[3 * channels :]
    first = nt(split[...], value)
    partial = first[:channels] + first[channels : 2 * channels] + first[2 * channels : 3 * channels]
    total = first[3 * channels : 3 * channels + 8]
    squares = (nt(ones, high) + nt(ones, low))[:8]
    blank = jnp.zeros((channels, LANES - rows), F32)
    scratch[...] = jnp.concatenate([partial, blank], axis=1) + consts[...]
    row = lax.broadcasted_iota(jnp.int32, (8, rows), 0)
    stats = jnp.concatenate([jnp.where(row == 0, total, squares), blank[:8]], axis=1)
    rank = lax.axis_index("tp")
    for i, out in enumerate(outs):
        block = rank ^ i
        for half in range(2):
            out[8 * half : 8 * half + 8] = scratch[pl.ds(pl.multiple_of((half * tp + block) * 8, 8), 8)]
        out[16:24] = stats


def total_kernel(own, *rest):
    arrived, (mine, other) = rest[:-2], rest[-2:]
    total = own[...]
    for block in arrived:
        total = total + block[...]
    half = lax.axis_index("cfg")
    first, second, stats = total[0:8], total[8:16], total[16:24]
    mine[0:8] = jnp.where(half == 0, first, second)
    mine[8:16] = stats
    other[0:8] = jnp.where(half == 0, second, first)
    other[8:16] = stats


def step_kernel(features, mine, theirs, coefs, out):
    rows = out.shape[1]

    def predict(block, consts):
        sums = block[0:8, :rows]
        mean = block[8:9, :rows] / features
        square = block[9:10, :rows] / features
        spread = lax.rsqrt(square - mean * mean + final_eps)
        return spread * (sums - mean * consts[0:8, rows : rows + 1]) + consts[0:8, rows + 1 : rows + 2]

    own, partner = predict(mine, mine), predict(theirs, mine)
    is_conditioned = lax.axis_index("cfg") == 0
    conditioned = jnp.where(is_conditioned, own, partner)
    unconditioned = jnp.where(is_conditioned, partner, own)
    guided = unconditioned + guide_scale * (conditioned - unconditioned)
    root_now, rest_now, root_next, rest_next, live, latents = (
        coefs[8 * i : 8 * i + 8, :rows] for i in range(6)
    )
    clean = root_now * latents - rest_now * guided
    noise = root_now * guided + rest_now * latents
    out[...] = jnp.where(live > 0.0, root_next * clean + rest_next * noise, 0.0)


def exchange(value, axis, distance):
    return lax.ppermute(value, axis, [(i, i ^ distance) for i in range(lax.axis_size(axis))])


def shards(
    stream, queries, keys, values, text_keys, text_values, out_weight, gate, shift, scale, proj_weight,
    q_gain, k_gain, lengths, latents, alphas, step_index,
):
    blocks = lax.axis_size("seq")
    tp = lax.axis_size("tp")
    rows, width = queries.shape[1:]
    columns = stream.shape[2]
    text = text_keys.shape[1]
    channels = proj_weight.shape[1]
    pairs = width // PAIR
    direct = blocks <= 4 and blocks & (blocks - 1) == 0

    q_gain, k_gain = q_gain.reshape(1, HEAD), k_gain.reshape(1, HEAD)
    packed = call(
        functools.partial(pack_keys_kernel, blocks), shape((rows, 2 * width), BF16), 4, smem=(0,), cost=2000000
    )(lengths, keys, values, k_gain)
    if direct:
        gathered = [packed] + [exchange(packed, "seq", d) for d in range(1, blocks)]
        order = lambda rank: [rank ^ d for d in range(blocks)]
    else:
        gathered = [lax.all_gather(packed, "seq", axis=0, tiled=True)]
        order = lambda rank: range(blocks)
    stacked, text_scores, bias = call(
        functools.partial(queries_kernel, blocks, order),
        [
            shape((pairs, 2 * rows, PAIR), BF16),
            shape((pairs, 2 * rows, text)),
            shape((1, blocks * rows)),
        ],
        5,
        smem=(0,),
        cost=20000000,
    )(lengths, queries, text_keys, q_gain, k_gain)
    sends = lambda rank: [rank ^ d for d in range(1, tp)]
    attended, *outgoing = call(
        functools.partial(attend_kernel, len(gathered), sends),
        [shape((rows, width), BF16)] + [shape((rows, columns), BF16)] * (tp - 1),
        5 + len(gathered),
        hbm=(4,),
        scratch=[pltpu.VMEM(out_weight.shape, BF16), pltpu.SemaphoreType.DMA],
        cost=100000000,
    )(stacked, text_scores, bias, text_values, out_weight, *gathered)
    arrived = [exchange(block, "tp", d) for d, block in enumerate(outgoing, 1)]
    base, factor, mask, split, consts, coefs = call(
        functools.partial(residual_kernel, tp),
        [
            shape((rows, columns)),
            shape((rows, columns)),
            shape((rows, LANES)),
            shape((3 * channels + 16, columns), BF16),
            shape((channels, LANES)),
            shape((48, LANES)),
        ],
        11,
        smem=(0, 1, 2),
        hbm=(4,),
        scratch=[pltpu.VMEM((width, columns), BF16), pltpu.SemaphoreType.DMA],
        cost=100000000,
    )(
        lengths, alphas, step_index, attended, out_weight, stream, gate.reshape(1, columns),
        shift.reshape(1, columns), scale.reshape(1, columns), proj_weight.T, latents.T,
    )
    hidden, *partials = call(
        functools.partial(hidden_kernel, tp),
        [shape((1, rows, columns), BF16)] + [shape((24, LANES))] * tp,
        5 + tp - 1,
        scratch=[pltpu.VMEM((channels, LANES), F32)],
        cost=20000000,
    )(base, factor, mask, split, consts, *arrived)
    shares = [exchange(block, "tp", d) for d, block in enumerate(partials) if d]
    mine, other = call(total_kernel, [shape((16, LANES))] * 2, tp)(partials[0], *shares)
    theirs = exchange(other, "cfg", 1)
    latents_out = call(
        functools.partial(step_kernel, columns * tp), shape((latents.shape[1], rows)), 3
    )(mine, theirs, coefs)
    return hidden, latents_out.T


def solution(mesh):
    return jax.shard_map(
        shards,
        mesh=mesh,
        in_specs=(
            P("cfg", "seq", "tp"),
            P("cfg", "seq", "tp"),
            P("cfg", "seq", "tp"),
            P("cfg", "seq", "tp"),
            P("cfg", None, "tp"),
            P("cfg", None, "tp"),
            P("tp", None),
            P("tp"),
            P("tp"),
            P("tp"),
            P("tp", None),
            P(),
            P(),
            P(),
            P("seq", ("cfg", "tp")),
            P(),
            P(),
        ),
        out_specs=(P("cfg", "seq", "tp"), P("seq", ("cfg", "tp"))),
        check_vma=False,
    )
```

```python
import functools
import math

import jax
import jax.numpy as jnp
from jax import lax
from jax.experimental import pallas as pl
from jax.experimental.pallas import tpu as pltpu
from jax.sharding import PartitionSpec as P

HEAD = 64
PAIR = 2 * HEAD
HP = 30
WP = 45
STRIDE = 20
LANES = 128

guide_scale = 6.0
head_eps = 1e-06
final_eps = 1e-05

F32 = jnp.float32
BF16 = jnp.bfloat16
VMEM_LIMIT = 24 * 1024 * 1024


def call(kernel, outs, ins, scratch=(), cost=0):
    spaces = {"v": pltpu.VMEM, "s": pltpu.SMEM, "h": pltpu.HBM}
    run = pl.pallas_call(
        kernel,
        out_shape=[o[0] for o in outs],
        in_specs=[pl.BlockSpec(memory_space=spaces[i]) for i in ins],
        out_specs=[pl.BlockSpec(memory_space=spaces[o[1]]) for o in outs],
        scratch_shapes=list(scratch),
        compiler_params=pltpu.CompilerParams(vmem_limit_bytes=VMEM_LIMIT),
        cost_estimate=pl.CostEstimate(flops=cost, bytes_accessed=cost // 64, transcendentals=0),
    )

    def placed(*operands):
        return run(
            *(
                pltpu.with_memory_space_constraint(x, pltpu.HBM) if i == "h" else x
                for i, x in zip(ins, operands, strict=True)
            )
        )

    return placed


def vmem(dims, dtype=F32):
    return jax.ShapeDtypeStruct(dims, dtype), "v"


def copies(sems, *pairs):
    started = [pltpu.make_async_copy(src, dst, sems.at[i]) for i, (src, dst) in enumerate(pairs)]
    for one in started:
        one.start()
    return started


def rows_of(parts, dtype):
    return jnp.concatenate([p.astype(F32) for p in parts], axis=0).astype(dtype)


def nt(left, right):
    return lax.dot_general(left, right, (((1,), (1,)), ((), ())), preferred_element_type=F32)


def nn(left, right):
    return jnp.dot(left, right, preferred_element_type=F32)


def prior(lengths, rank, blocks):
    total = jnp.int32(0)
    for i in range(blocks):
        total = total + jnp.where(i < rank, lengths[i], 0)
    return total


def averager():
    row = lax.broadcasted_iota(jnp.int32, (PAIR, PAIR), 0)
    col = lax.broadcasted_iota(jnp.int32, (PAIR, PAIR), 1)
    return jnp.where((row < HEAD) == (col < HEAD), 1.0 / HEAD, 0.0).astype(BF16)


def head_norm(field, average, gain):
    centre = field.astype(F32) - nn(field, average)
    square = centre * centre
    high = square.astype(BF16)
    low = (square - high.astype(F32)).astype(BF16)
    spread = nn(high, average) + nn(low, average)
    return centre * lax.rsqrt(spread + head_eps) * gain


def rope_tables(start, rows):
    lane = lax.broadcasted_iota(jnp.int32, (rows, PAIR), 1)
    pos = (lax.broadcasted_iota(jnp.int32, (rows, PAIR), 0) + start).astype(F32)
    frame = jnp.floor((pos + 0.5) * (1.0 / (HP * WP)))
    line = jnp.floor((pos + 0.5) * (1.0 / WP))
    across = pos - line * WP
    height = line - frame * HP
    pair = (lane % HEAD) // 2
    in_frame = pair < 8
    in_height = pair < 20
    coord = jnp.where(in_frame, frame, jnp.where(in_height, height, across))
    step = jnp.where(in_frame, pair, jnp.where(in_height, pair - 8, pair - 20)).astype(F32)
    rate = jnp.where(in_frame, 2.0 / 16, 2.0 / 24)
    angle = coord * jnp.exp(step * rate * (-math.log(10000.0)))
    sine = jnp.sin(angle)
    return jnp.cos(angle), jnp.where(lane % 2 == 0, -sine, sine)


def rotate(field, cos_table, sin_table):
    even = lax.broadcasted_iota(jnp.int32, field.shape, 1) % 2 == 0
    other = jnp.where(even, pltpu.roll(field, PAIR - 1, 1), pltpu.roll(field, 1, 1))
    return field * cos_table + other * sin_table


def twice(gain_ref):
    gain = gain_ref[...]
    return jnp.concatenate([gain, gain], axis=1)


def pack_keys_kernel(blocks, lengths_at, keys_at, values_at, gain_at, packed, lengths, keys, values, gain, sems):
    arriving = copies(sems, (lengths_at, lengths), (keys_at, keys), (gain_at, gain), (values_at, values))
    rows, width = keys.shape[1:]
    average = averager()
    arriving[0].wait()
    tables = rope_tables(prior(lengths, lax.axis_index("seq"), blocks), rows)
    arriving[1].wait()
    arriving[2].wait()
    wide = twice(gain)
    for at in range(0, width, PAIR):
        normed = head_norm(keys[0, :, at : at + PAIR], average, wide)
        packed[:, at : at + PAIR] = rotate(normed, *tables).astype(BF16)
    arriving[3].wait()
    packed[:, width:] = values[0]


def queries_kernel(
    blocks, order, lengths_at, queries_at, text_keys_at, q_gain_at, k_gain_at, text_values_at, weight_at,
    stacked, text_scores, bias, text_values, weight, lengths, queries, text_keys, q_gain, k_gain, sems,
):
    arriving = copies(
        sems, (lengths_at, lengths), (queries_at, queries), (q_gain_at, q_gain), (k_gain_at, k_gain),
        (text_keys_at, text_keys), (text_values_at, text_values), (weight_at, weight),
    )
    rows, width = queries.shape[1:]
    rank = lax.axis_index("seq")
    average = averager()
    left = lax.broadcasted_iota(jnp.int32, (rows, PAIR), 1) < HEAD
    lane = lax.broadcasted_iota(jnp.int32, bias.shape, 1)
    live = lane < 0
    arriving[0].wait()
    for i, block in enumerate(order(rank)):
        live = live | ((lane >= i * rows) & (lane < i * rows + lengths[block]))
    bias[...] = jnp.where(live, 0.0, -jnp.inf)
    tables = rope_tables(prior(lengths, rank, blocks), rows)
    for one in arriving[1:5]:
        one.wait()
    q_wide, k_wide = twice(q_gain), twice(k_gain)
    for p, at in enumerate(range(0, width, PAIR)):
        query = rotate(head_norm(queries[0, :, at : at + PAIR], average, q_wide), *tables)
        query = query.astype(BF16).astype(F32) * 0.125
        both = jnp.concatenate([jnp.where(left, query, 0.0), jnp.where(left, 0.0, query)], axis=0)
        both = both.astype(BF16)
        stacked[p] = both
        key = head_norm(text_keys[0, :, at : at + PAIR], average, k_wide).astype(BF16)
        text_scores[p] = nt(both, key)
    arriving[5].wait()
    arriving[6].wait()


def attend_kernel(n_blocks, sends, stacked, text_scores, bias, text_values, weight, *rest):
    gathered, attended, outs = rest[:n_blocks], rest[n_blocks], rest[n_blocks + 1 :]
    pairs, double = stacked.shape[:2]
    rows, width = double // 2, pairs * PAIR
    if n_blocks > 1:
        video = rows_of([g[...] for g in gathered], BF16)
    else:
        video = gathered[0][...]
    left = lax.broadcasted_iota(jnp.int32, (rows, PAIR), 1) < HEAD
    parts = []
    for p in range(pairs):
        at = p * PAIR
        scores_t = text_scores[p]
        scores_v = nt(stacked[p], video[:, at : at + PAIR]) + bias[...]
        row_max = jnp.maximum(
            jnp.max(scores_t, axis=1, keepdims=True), jnp.max(scores_v, axis=1, keepdims=True)
        )
        weights_t = jnp.exp(scores_t - row_max)
        weights_v = jnp.exp(scores_v - row_max)
        totals = jnp.sum(weights_t, axis=1, keepdims=True) + jnp.sum(weights_v, axis=1, keepdims=True)
        mixed = nn(weights_t.astype(BF16), text_values[0, :, at : at + PAIR])
        mixed = mixed + nn(weights_v.astype(BF16), video[:, width + at : width + at + PAIR])
        mixed = mixed / totals
        parts.append(jnp.where(left, mixed[:rows], mixed[rows:]).astype(BF16))
    joined = jnp.concatenate(parts, axis=1)
    attended[...] = joined
    project(sends, joined, weight, outs)


def project(sends, joined, weight, outs):
    for out, block in zip(outs, sends(lax.axis_index("tp"))):
        columns = out.shape[1]
        at = pl.multiple_of(block * columns, columns)
        out[...] = nn(joined, weight[:, pl.ds(at, columns)]).astype(out.dtype)


def project_kernel(sends, attended, weight, *outs):
    project(sends, attended[...], weight, outs)


def keep_kernel(value, out, sem):
    (one,) = copies(sem, (value, out.at[0]))
    one.wait()


def residual_kernel(
    tp, lengths, alphas, step, attended, weight, stream, gate, shift, scale, proj, latents,
    base, factor, split, consts, coefs,
):
    rank = lax.axis_index("tp")
    rows, columns = base.shape
    count = lengths[lax.axis_index("seq")]
    alive = lax.broadcasted_iota(jnp.int32, (rows, 1), 0) < count
    factor[...] = jnp.where(alive, gate[...], 0.0)
    channels = proj.shape[0]
    plain = proj[...]
    scaled = plain * (1.0 + scale[...])
    high = scaled.astype(BF16)
    rest = scaled - high.astype(F32)
    middle = rest.astype(BF16)
    split[0:channels] = high
    split[channels : 2 * channels] = middle
    split[2 * channels : 3 * channels] = (rest - middle.astype(F32)).astype(BF16)
    split[3 * channels :] = jnp.ones((16, columns), BF16)
    lane = lax.broadcasted_iota(jnp.int32, consts.shape, 1)
    consts[...] = jnp.where(
        lane == rows,
        jnp.sum(scaled, axis=1, keepdims=True),
        jnp.where(lane == rows + 1, jnp.sum(plain * shift[...], axis=1, keepdims=True), 0.0),
    )
    at = step[0]
    now = jnp.full((8, LANES), alphas[at], F32)
    earlier = jnp.full((8, LANES), alphas[at - STRIDE], F32)
    coefs[0:8] = jnp.sqrt(now)
    coefs[8:16] = jnp.sqrt(1.0 - now)
    coefs[16:24] = jnp.sqrt(earlier)
    coefs[24:32] = jnp.sqrt(1.0 - earlier)
    lane8 = lax.broadcasted_iota(jnp.int32, (8, LANES), 1)
    coefs[32:40] = jnp.where(lane8 < count, 1.0, 0.0)
    coefs[40:48] = jnp.concatenate([latents[...], jnp.zeros((8, LANES - rows), F32)], axis=1)
    own = nn(attended[...], weight[:, pl.ds(pl.multiple_of(rank * columns, columns), columns)])
    base[...] = jnp.where(alive, stream[0].astype(F32) + gate[...] * own, 0.0)


def hidden_kernel(tp, base, factor, split, consts, *rest):
    arrived, (hidden, *outs), scratch = rest[: tp - 1], rest[tp - 1 : -1], rest[-1]
    summed = arrived[0][...].astype(F32)
    for block in arrived[1:]:
        summed = summed + block[...].astype(F32)
    value = (base[...] + factor[...] * summed).astype(BF16)
    hidden[...] = value
    rows = value.shape[0]
    channels = consts.shape[0]
    wide = value.astype(F32)
    square = wide * wide
    high = square.astype(BF16)
    low = (square - high.astype(F32)).astype(BF16)
    ones = split[3 * channels :]
    first = nt(split[...], value)
    partial = first[:channels] + first[channels : 2 * channels] + first[2 * channels : 3 * channels]
    total = first[3 * channels : 3 * channels + 8]
    squares = (nt(ones, high) + nt(ones, low))[:8]
    blank = jnp.zeros((channels, LANES - rows), F32)
    scratch[...] = jnp.concatenate([partial, blank], axis=1) + consts[...]
    row = lax.broadcasted_iota(jnp.int32, (8, rows), 0)
    stats = jnp.concatenate([jnp.where(row == 0, total, squares), blank[:8]], axis=1)
    rank = lax.axis_index("tp")
    for i, out in enumerate(outs):
        block = rank ^ i
        for half in range(2):
            out[8 * half : 8 * half + 8] = scratch[pl.ds(pl.multiple_of((half * tp + block) * 8, 8), 8)]
        out[16:24] = stats


def total_kernel(own, *rest):
    arrived, (mine, other) = rest[:-2], rest[-2:]
    total = own[...]
    for block in arrived:
        total = total + block[...]
    half = lax.axis_index("cfg")
    first, second, stats = total[0:8], total[8:16], total[16:24]
    mine[0:8] = jnp.where(half == 0, first, second)
    mine[8:16] = stats
    other[0:8] = jnp.where(half == 0, second, first)
    other[8:16] = stats


def step_kernel(features, mine, theirs, coefs, out):
    rows = out.shape[1]

    def predict(block, consts):
        sums = block[0:8, :rows]
        mean = block[8:9, :rows] / features
        square = block[9:10, :rows] / features
        spread = lax.rsqrt(square - mean * mean + final_eps)
        return spread * (sums - mean * consts[0:8, rows : rows + 1]) + consts[0:8, rows + 1 : rows + 2]

    own, partner = predict(mine, mine), predict(theirs, mine)
    is_conditioned = lax.axis_index("cfg") == 0
    conditioned = jnp.where(is_conditioned, own, partner)
    unconditioned = jnp.where(is_conditioned, partner, own)
    guided = unconditioned + guide_scale * (conditioned - unconditioned)
    root_now, rest_now, root_next, rest_next, live, latents = (
        coefs[8 * i : 8 * i + 8, :rows] for i in range(6)
    )
    clean = root_now * latents - rest_now * guided
    noise = root_now * guided + rest_now * latents
    out[...] = jnp.where(live > 0.0, root_next * clean + rest_next * noise, 0.0)


def exchange(value, axis, distance):
    return lax.ppermute(value, axis, [(i, i ^ distance) for i in range(lax.axis_size(axis))])


def shards(
    stream, queries, keys, values, text_keys, text_values, out_weight, gate, shift, scale, proj_weight,
    q_gain, k_gain, lengths, latents, alphas, step_index,
):
    blocks = lax.axis_size("seq")
    tp = lax.axis_size("tp")
    rows, width = queries.shape[1:]
    columns = stream.shape[2]
    text = text_keys.shape[1]
    channels = proj_weight.shape[1]
    pairs = width // PAIR
    direct = blocks <= 4 and blocks & (blocks - 1) == 0
    q_gain, k_gain = q_gain.reshape(1, HEAD), k_gain.reshape(1, HEAD)
    one_gain = pltpu.VMEM(q_gain.shape, F32)
    counts = pltpu.SMEM(lengths.shape, jnp.int32)

    (packed,) = call(
        functools.partial(pack_keys_kernel, blocks),
        [vmem((rows, 2 * width), BF16)],
        "hhhh",
        [counts, pltpu.VMEM(keys.shape, BF16), pltpu.VMEM(values.shape, BF16), one_gain, pltpu.SemaphoreType.DMA((4,))],
        cost=2000000,
    )(lengths, keys, values, k_gain)
    if direct:
        gathered = [packed] + [exchange(packed, "seq", d) for d in range(1, blocks)]
        order = lambda rank: [rank ^ d for d in range(blocks)]
    else:
        gathered = [lax.all_gather(packed, "seq", axis=0, tiled=True)]
        order = lambda rank: range(blocks)
    stacked, text_scores, bias, held_values, held_weight = call(
        functools.partial(queries_kernel, blocks, order),
        [
            vmem((pairs, 2 * rows, PAIR), BF16),
            vmem((pairs, 2 * rows, text)),
            vmem((1, blocks * rows)),
            vmem(text_values.shape, BF16),
            vmem(out_weight.shape, BF16),
        ],
        "hhhhhhh",
        [
            counts, pltpu.VMEM(queries.shape, BF16), pltpu.VMEM(text_keys.shape, BF16), one_gain, one_gain,
            pltpu.SemaphoreType.DMA((7,)),
        ],
        cost=20000000,
    )(lengths, queries, text_keys, q_gain, k_gain, text_values, out_weight)
    partners = list(range(tp - 1, 0, -1))
    attended, *outgoing = call(
        functools.partial(attend_kernel, len(gathered), lambda rank: [rank ^ d for d in partners]),
        [vmem((rows, width), BF16)] + [vmem((rows, columns), BF16)] * (tp - 1),
        "v" * (5 + len(gathered)),
        cost=100000000,
    )(stacked, text_scores, bias, held_values, held_weight, *gathered)
    arrived = [exchange(block, "tp", d) for d, block in zip(partners, outgoing)]
    base, factor, split, consts, coefs = call(
        functools.partial(residual_kernel, tp),
        [
            vmem((rows, columns)),
            vmem((rows, columns)),
            vmem((3 * channels + 16, columns), BF16),
            vmem((channels, LANES)),
            vmem((48, LANES)),
        ],
        "sss" + "v" * 8,
        cost=100000000,
    )(
        lengths, alphas, step_index, attended, held_weight, stream, gate.reshape(1, columns),
        shift.reshape(1, columns), scale.reshape(1, columns), proj_weight.T, latents.T,
    )
    hidden, *partials = call(
        functools.partial(hidden_kernel, tp),
        [vmem((rows, columns), BF16)] + [vmem((24, LANES))] * tp,
        "v" * (4 + tp - 1),
        [pltpu.VMEM((channels, LANES), F32)],
        cost=20000000,
    )(base, factor, split, consts, *arrived)
    shares = [exchange(partials[d], "tp", d) for d in partners]
    (hidden_out,) = call(
        keep_kernel, [(jax.ShapeDtypeStruct(stream.shape, BF16), "h")], "v", [pltpu.SemaphoreType.DMA((1,))], cost=2000000
    )(hidden)
    mine, other = call(total_kernel, [vmem((16, LANES))] * 2, "v" * tp)(partials[0], *shares)
    theirs = exchange(other, "cfg", 1)
    (latents_out,) = call(
        functools.partial(step_kernel, columns * tp), [vmem((latents.shape[1], rows))], "vvv"
    )(mine, theirs, coefs)
    return hidden_out, latents_out.T


def solution(mesh):
    return jax.shard_map(
        shards,
        mesh=mesh,
        in_specs=(
            P("cfg", "seq", "tp"),
            P("cfg", "seq", "tp"),
            P("cfg", "seq", "tp"),
            P("cfg", "seq", "tp"),
            P("cfg", None, "tp"),
            P("cfg", None, "tp"),
            P("tp", None),
            P("tp"),
            P("tp"),
            P("tp"),
            P("tp", None),
            P(),
            P(),
            P(),
            P("seq", ("cfg", "tp")),
            P(),
            P(),
        ),
        out_specs=(P("cfg", "seq", "tp"), P("seq", ("cfg", "tp"))),
        check_vma=False,
    )
```

```python
import functools
import math

import jax
import jax.numpy as jnp
from jax import lax
from jax.experimental import pallas as pl
from jax.experimental.pallas import tpu as pltpu
from jax.sharding import PartitionSpec as P

HEAD = 64
PAIR = 2 * HEAD
HP = 30
WP = 45
STRIDE = 20
LANES = 128

guide_scale = 6.0
head_eps = 1e-06
final_eps = 1e-05

F32 = jnp.float32
BF16 = jnp.bfloat16
VMEM_LIMIT = 24 * 1024 * 1024


def call(kernel, outs, ins, scratch=(), cost=0):
    spaces = {"v": pltpu.VMEM, "s": pltpu.SMEM, "h": pltpu.HBM}
    run = pl.pallas_call(
        kernel,
        out_shape=[o[0] for o in outs],
        in_specs=[pl.BlockSpec(memory_space=spaces[i]) for i in ins],
        out_specs=[pl.BlockSpec(memory_space=spaces[o[1]]) for o in outs],
        scratch_shapes=list(scratch),
        compiler_params=pltpu.CompilerParams(vmem_limit_bytes=VMEM_LIMIT),
        cost_estimate=pl.CostEstimate(flops=cost, bytes_accessed=cost // 64, transcendentals=0),
    )

    def placed(*operands):
        return run(
            *(
                pltpu.with_memory_space_constraint(x, pltpu.HBM) if i == "h" else x
                for i, x in zip(ins, operands, strict=True)
            )
        )

    return placed


def vmem(dims, dtype=F32):
    return jax.ShapeDtypeStruct(dims, dtype), "v"


def copies(sems, *pairs):
    started = [pltpu.make_async_copy(src, dst, sems.at[i]) for i, (src, dst) in enumerate(pairs)]
    for one in started:
        one.start()
    return started


def rows_of(parts, dtype):
    return jnp.concatenate([p.astype(F32) for p in parts], axis=0).astype(dtype)


def nt(left, right):
    return lax.dot_general(left, right, (((1,), (1,)), ((), ())), preferred_element_type=F32)


def nn(left, right):
    return jnp.dot(left, right, preferred_element_type=F32)


def prior(lengths, rank, blocks):
    total = jnp.int32(0)
    for i in range(blocks):
        total = total + jnp.where(i < rank, lengths[i], 0)
    return total


def averager():
    row = lax.broadcasted_iota(jnp.int32, (PAIR, PAIR), 0)
    col = lax.broadcasted_iota(jnp.int32, (PAIR, PAIR), 1)
    return jnp.where((row < HEAD) == (col < HEAD), 1.0 / HEAD, 0.0).astype(BF16)


def head_norm(field, average, gain):
    centre = field.astype(F32) - nn(field, average)
    square = centre * centre
    high = square.astype(BF16)
    low = (square - high.astype(F32)).astype(BF16)
    spread = nn(high, average) + nn(low, average)
    return centre * lax.rsqrt(spread + head_eps) * gain


def rope_tables(start, rows):
    lane = lax.broadcasted_iota(jnp.int32, (rows, PAIR), 1)
    pos = (lax.broadcasted_iota(jnp.int32, (rows, PAIR), 0) + start).astype(F32)
    frame = jnp.floor((pos + 0.5) * (1.0 / (HP * WP)))
    line = jnp.floor((pos + 0.5) * (1.0 / WP))
    across = pos - line * WP
    height = line - frame * HP
    pair = (lane % HEAD) // 2
    in_frame = pair < 8
    in_height = pair < 20
    coord = jnp.where(in_frame, frame, jnp.where(in_height, height, across))
    step = jnp.where(in_frame, pair, jnp.where(in_height, pair - 8, pair - 20)).astype(F32)
    rate = jnp.where(in_frame, 2.0 / 16, 2.0 / 24)
    angle = coord * jnp.exp(step * rate * (-math.log(10000.0)))
    sine = jnp.sin(angle)
    return jnp.cos(angle), jnp.where(lane % 2 == 0, -sine, sine)


def rotate(field, cos_table, sin_table):
    even = lax.broadcasted_iota(jnp.int32, field.shape, 1) % 2 == 0
    other = jnp.where(even, pltpu.roll(field, PAIR - 1, 1), pltpu.roll(field, 1, 1))
    return field * cos_table + other * sin_table


def twice(gain_ref):
    gain = gain_ref[...]
    return jnp.concatenate([gain, gain], axis=1)


def pack_keys_kernel(blocks, lengths_at, keys_at, values_at, gain_at, packed, lengths, keys, values, gain, sems):
    arriving = copies(sems, (lengths_at, lengths), (keys_at, keys), (gain_at, gain), (values_at, values))
    rows, width = keys.shape[1:]
    average = averager()
    arriving[0].wait()
    tables = rope_tables(prior(lengths, lax.axis_index("seq"), blocks), rows)
    arriving[1].wait()
    arriving[2].wait()
    wide = twice(gain)
    for at in range(0, width, PAIR):
        normed = head_norm(keys[0, :, at : at + PAIR], average, wide)
        packed[:, at : at + PAIR] = rotate(normed, *tables).astype(BF16)
    arriving[3].wait()
    packed[:, width:] = values[0]


def queries_kernel(
    blocks, order, lengths_at, queries_at, text_keys_at, q_gain_at, k_gain_at, text_values_at, weight_at,
    stacked, text_scores, bias, text_values, weight, lengths, queries, text_keys, q_gain, k_gain, sems,
):
    arriving = copies(
        sems, (lengths_at, lengths), (queries_at, queries), (q_gain_at, q_gain), (k_gain_at, k_gain),
        (text_keys_at, text_keys), (text_values_at, text_values), (weight_at, weight),
    )
    rows, width = queries.shape[1:]
    rank = lax.axis_index("seq")
    average = averager()
    left = lax.broadcasted_iota(jnp.int32, (rows, PAIR), 1) < HEAD
    lane = lax.broadcasted_iota(jnp.int32, bias.shape, 1)
    live = lane < 0
    arriving[0].wait()
    for i, block in enumerate(order(rank)):
        live = live | ((lane >= i * rows) & (lane < i * rows + lengths[block]))
    bias[...] = jnp.where(live, 0.0, -jnp.inf)
    tables = rope_tables(prior(lengths, rank, blocks), rows)
    for one in arriving[1:5]:
        one.wait()
    q_wide, k_wide = twice(q_gain), twice(k_gain)
    for p, at in enumerate(range(0, width, PAIR)):
        query = rotate(head_norm(queries[0, :, at : at + PAIR], average, q_wide), *tables)
        query = query.astype(BF16).astype(F32) * 0.125
        both = jnp.concatenate([jnp.where(left, query, 0.0), jnp.where(left, 0.0, query)], axis=0)
        both = both.astype(BF16)
        stacked[p] = both
        key = head_norm(text_keys[0, :, at : at + PAIR], average, k_wide).astype(BF16)
        text_scores[p] = nt(both, key)
    arriving[5].wait()
    arriving[6].wait()


def attend_kernel(n_blocks, sends, stacked, text_scores, bias, text_values, weight, *rest):
    gathered, attended, outs = rest[:n_blocks], rest[n_blocks], rest[n_blocks + 1 :]
    pairs, double = stacked.shape[:2]
    rows, width = double // 2, pairs * PAIR
    if n_blocks > 1:
        video = rows_of([g[...] for g in gathered], BF16)
    else:
        video = gathered[0][...]
    left = lax.broadcasted_iota(jnp.int32, (rows, PAIR), 1) < HEAD
    parts = []
    for p in range(pairs):
        at = p * PAIR
        scores_t = text_scores[p]
        scores_v = nt(stacked[p], video[:, at : at + PAIR]) + bias[...]
        row_max = jnp.maximum(
            jnp.max(scores_t, axis=1, keepdims=True), jnp.max(scores_v, axis=1, keepdims=True)
        )
        weights_t = jnp.exp(scores_t - row_max)
        weights_v = jnp.exp(scores_v - row_max)
        totals = jnp.sum(weights_t, axis=1, keepdims=True) + jnp.sum(weights_v, axis=1, keepdims=True)
        mixed = nn(weights_t.astype(BF16), text_values[0, :, at : at + PAIR])
        mixed = mixed + nn(weights_v.astype(BF16), video[:, width + at : width + at + PAIR])
        mixed = mixed / totals
        parts.append(jnp.where(left, mixed[:rows], mixed[rows:]).astype(BF16))
    joined = jnp.concatenate(parts, axis=1)
    attended[...] = joined
    project(sends, joined, weight, outs)


def project(sends, joined, weight, outs):
    for out, block in zip(outs, sends(lax.axis_index("tp"))):
        columns = out.shape[1]
        at = pl.multiple_of(block * columns, columns)
        out[...] = nn(joined, weight[:, pl.ds(at, columns)]).astype(out.dtype)


def project_kernel(sends, attended, weight, *outs):
    project(sends, attended[...], weight, outs)


def keep_kernel(value, out, sem):
    (one,) = copies(sem, (value, out.at[0]))
    one.wait()


def residual_kernel(
    tp, lengths, alphas, step, attended, weight, stream, gate, shift, scale, proj, latents,
    base, factor, split, consts, coefs,
):
    rank = lax.axis_index("tp")
    rows, columns = base.shape
    count = lengths[lax.axis_index("seq")]
    alive = lax.broadcasted_iota(jnp.int32, (rows, 1), 0) < count
    factor[...] = jnp.where(alive, gate[...], 0.0)
    channels = proj.shape[0]
    plain = proj[...]
    scaled = plain * (1.0 + scale[...])
    high = scaled.astype(BF16)
    rest = scaled - high.astype(F32)
    middle = rest.astype(BF16)
    split[0:channels] = high
    split[channels : 2 * channels] = middle
    split[2 * channels : 3 * channels] = (rest - middle.astype(F32)).astype(BF16)
    split[3 * channels :] = jnp.ones((16, columns), BF16)
    lane = lax.broadcasted_iota(jnp.int32, consts.shape, 1)
    consts[...] = jnp.where(
        lane == rows,
        jnp.sum(scaled, axis=1, keepdims=True),
        jnp.where(lane == rows + 1, jnp.sum(plain * shift[...], axis=1, keepdims=True), 0.0),
    )
    at = step[0]
    now = jnp.full((8, LANES), alphas[at], F32)
    earlier = jnp.full((8, LANES), alphas[at - STRIDE], F32)
    coefs[0:8] = jnp.sqrt(now)
    coefs[8:16] = jnp.sqrt(1.0 - now)
    coefs[16:24] = jnp.sqrt(earlier)
    coefs[24:32] = jnp.sqrt(1.0 - earlier)
    lane8 = lax.broadcasted_iota(jnp.int32, (8, LANES), 1)
    coefs[32:40] = jnp.where(lane8 < count, 1.0, 0.0)
    coefs[40:48] = jnp.concatenate([latents[...], jnp.zeros((8, LANES - rows), F32)], axis=1)
    own = nn(attended[...], weight[:, pl.ds(pl.multiple_of(rank * columns, columns), columns)])
    base[...] = jnp.where(alive, stream[0].astype(F32) + gate[...] * own, 0.0)


def hidden_kernel(tp, routes, base, factor, split, consts, *rest):
    arrived, (hidden, *outs), scratch = rest[: tp - 1], rest[tp - 1 : -1], rest[-1]
    summed = arrived[0][...].astype(F32)
    for block in arrived[1:]:
        summed = summed + block[...].astype(F32)
    value = (base[...] + factor[...] * summed).astype(BF16)
    hidden[...] = value
    rows = value.shape[0]
    channels = consts.shape[0]
    wide = value.astype(F32)
    square = wide * wide
    high = square.astype(BF16)
    low = (square - high.astype(F32)).astype(BF16)
    ones = split[3 * channels :]
    first = nt(split[...], value)
    partial = first[:channels] + first[channels : 2 * channels] + first[2 * channels : 3 * channels]
    total = first[3 * channels : 3 * channels + 8]
    squares = (nt(ones, high) + nt(ones, low))[:8]
    blank = jnp.zeros((channels, LANES - rows), F32)
    scratch[...] = jnp.concatenate([partial, blank], axis=1) + consts[...]
    row = lax.broadcasted_iota(jnp.int32, (8, rows), 0)
    stats = jnp.concatenate([jnp.where(row == 0, total, squares), blank[:8]], axis=1)
    rank = lax.axis_index("tp")
    for i, out in enumerate(outs):
        block = entry(routes[i], rank)
        for half in range(2):
            out[8 * half : 8 * half + 8] = scratch[pl.ds(pl.multiple_of((half * tp + block) * 8, 8), 8)]
        out[16:24] = stats


def total_kernel(own, *rest):
    arrived, (mine, other) = rest[:-2], rest[-2:]
    total = own[...]
    for block in arrived:
        total = total + block[...]
    half = lax.axis_index("cfg")
    first, second, stats = total[0:8], total[8:16], total[16:24]
    mine[0:8] = jnp.where(half == 0, first, second)
    mine[8:16] = stats
    other[0:8] = jnp.where(half == 0, second, first)
    other[8:16] = stats


def step_kernel(features, mine, theirs, coefs, out):
    rows = out.shape[1]

    def predict(block, consts):
        sums = block[0:8, :rows]
        mean = block[8:9, :rows] / features
        square = block[9:10, :rows] / features
        spread = lax.rsqrt(square - mean * mean + final_eps)
        return spread * (sums - mean * consts[0:8, rows : rows + 1]) + consts[0:8, rows + 1 : rows + 2]

    own, partner = predict(mine, mine), predict(theirs, mine)
    is_conditioned = lax.axis_index("cfg") == 0
    conditioned = jnp.where(is_conditioned, own, partner)
    unconditioned = jnp.where(is_conditioned, partner, own)
    guided = unconditioned + guide_scale * (conditioned - unconditioned)
    root_now, rest_now, root_next, rest_next, live, latents = (
        coefs[8 * i : 8 * i + 8, :rows] for i in range(6)
    )
    clean = root_now * latents - rest_now * guided
    noise = root_now * guided + rest_now * latents
    out[...] = jnp.where(live > 0.0, root_next * clean + rest_next * noise, 0.0)


def exchange(value, axis, distance):
    return lax.ppermute(value, axis, [(i, i ^ distance) for i in range(lax.axis_size(axis))])


def send(value, axis, route):
    return lax.ppermute(value, axis, list(enumerate(route)))


def entry(route, rank):
    place = jnp.int32(route[0])
    for i, to in enumerate(route[1:], 1):
        place = jnp.where(rank == i, to, place)
    return place


def shards(
    stream, queries, keys, values, text_keys, text_values, out_weight, gate, shift, scale, proj_weight,
    q_gain, k_gain, lengths, latents, alphas, step_index,
):
    blocks = lax.axis_size("seq")
    tp = lax.axis_size("tp")
    rows, width = queries.shape[1:]
    columns = stream.shape[2]
    text = text_keys.shape[1]
    channels = proj_weight.shape[1]
    pairs = width // PAIR
    direct = blocks <= 4 and blocks & (blocks - 1) == 0
    q_gain, k_gain = q_gain.reshape(1, HEAD), k_gain.reshape(1, HEAD)
    one_gain = pltpu.VMEM(q_gain.shape, F32)
    counts = pltpu.SMEM(lengths.shape, jnp.int32)

    (packed,) = call(
        functools.partial(pack_keys_kernel, blocks),
        [vmem((rows, 2 * width), BF16)],
        "hhhh",
        [counts, pltpu.VMEM(keys.shape, BF16), pltpu.VMEM(values.shape, BF16), one_gain, pltpu.SemaphoreType.DMA((4,))],
        cost=2000000,
    )(lengths, keys, values, k_gain)
    if direct:
        gathered = [packed] + [exchange(packed, "seq", d) for d in (3, 2, 1)]
        order = lambda rank: [rank] + [rank ^ d for d in (3, 2, 1)]
    else:
        gathered = [lax.all_gather(packed, "seq", axis=0, tiled=True)]
        order = lambda rank: range(blocks)
    stacked, text_scores, bias, held_values, held_weight = call(
        functools.partial(queries_kernel, blocks, order),
        [
            vmem((pairs, 2 * rows, PAIR), BF16),
            vmem((pairs, 2 * rows, text)),
            vmem((1, blocks * rows)),
            vmem(text_values.shape, BF16),
            vmem(out_weight.shape, BF16),
        ],
        "hhhhhhh",
        [
            counts, pltpu.VMEM(queries.shape, BF16), pltpu.VMEM(text_keys.shape, BF16), one_gain, one_gain,
            pltpu.SemaphoreType.DMA((7,)),
        ],
        cost=20000000,
    )(lengths, queries, text_keys, q_gain, k_gain, text_values, out_weight)
    routes = [[i ^ d for i in range(tp)] for d in range(tp - 1, 0, -1)]
    late_routes = routes
    attended, *outgoing = call(
        functools.partial(attend_kernel, len(gathered), lambda rank: [entry(r, rank) for r in routes]),
        [vmem((rows, width), BF16)] + [vmem((rows, columns), BF16)] * (tp - 1),
        "v" * (5 + len(gathered)),
        cost=100000000,
    )(stacked, text_scores, bias, held_values, held_weight, *gathered)
    arrived = [send(block, "tp", r) for r, block in zip(routes, outgoing)]
    base, factor, split, consts, coefs = call(
        functools.partial(residual_kernel, tp),
        [
            vmem((rows, columns)),
            vmem((rows, columns)),
            vmem((3 * channels + 16, columns), BF16),
            vmem((channels, LANES)),
            vmem((48, LANES)),
        ],
        "sss" + "v" * 8,
        cost=100000000,
    )(
        lengths, alphas, step_index, attended, held_weight, stream, gate.reshape(1, columns),
        shift.reshape(1, columns), scale.reshape(1, columns), proj_weight.T, latents.T,
    )
    hidden, *partials = call(
        functools.partial(hidden_kernel, tp, [list(range(tp))] + late_routes),
        [vmem((rows, columns), BF16)] + [vmem((24, LANES))] * tp,
        "v" * (4 + tp - 1),
        [pltpu.VMEM((channels, LANES), F32)],
        cost=20000000,
    )(base, factor, split, consts, *arrived)
    shares = [send(block, "tp", r) for r, block in zip(late_routes, partials[1:])]
    (hidden_out,) = call(
        keep_kernel, [(jax.ShapeDtypeStruct(stream.shape, BF16), "h")], "v", [pltpu.SemaphoreType.DMA((1,))], cost=2000000
    )(hidden)
    mine, other = call(total_kernel, [vmem((16, LANES))] * 2, "v" * tp)(partials[0], *shares)
    theirs = exchange(other, "cfg", 1)
    (latents_out,) = call(
        functools.partial(step_kernel, columns * tp), [vmem((latents.shape[1], rows))], "vvv"
    )(mine, theirs, coefs)
    return hidden_out, latents_out.T


def solution(mesh):
    return jax.shard_map(
        shards,
        mesh=mesh,
        in_specs=(
            P("cfg", "seq", "tp"),
            P("cfg", "seq", "tp"),
            P("cfg", "seq", "tp"),
            P("cfg", "seq", "tp"),
            P("cfg", None, "tp"),
            P("cfg", None, "tp"),
            P("tp", None),
            P("tp"),
            P("tp"),
            P("tp"),
            P("tp", None),
            P(),
            P(),
            P(),
            P("seq", ("cfg", "tp")),
            P(),
            P(),
        ),
        out_specs=(P("cfg", "seq", "tp"), P("seq", ("cfg", "tp"))),
        check_vma=False,
    )
```

```python
import functools
import math

import jax
import jax.numpy as jnp
from jax import lax
from jax.experimental import pallas as pl
from jax.experimental.pallas import tpu as pltpu
from jax.sharding import PartitionSpec as P

HEAD = 64
PAIR = 2 * HEAD
HP = 30
WP = 45
STRIDE = 20
LANES = 128

guide_scale = 6.0
head_eps = 1e-06
final_eps = 1e-05

F32 = jnp.float32
BF16 = jnp.bfloat16
VMEM_LIMIT = 24 * 1024 * 1024


def call(kernel, outs, ins, scratch=(), cost=0):
    spaces = {"v": pltpu.VMEM, "s": pltpu.SMEM, "h": pltpu.HBM}
    run = pl.pallas_call(
        kernel,
        out_shape=[o[0] for o in outs],
        in_specs=[pl.BlockSpec(memory_space=spaces[i]) for i in ins],
        out_specs=[pl.BlockSpec(memory_space=spaces[o[1]]) for o in outs],
        scratch_shapes=list(scratch),
        compiler_params=pltpu.CompilerParams(vmem_limit_bytes=VMEM_LIMIT),
        cost_estimate=pl.CostEstimate(flops=cost, bytes_accessed=cost // 64, transcendentals=0),
    )

    def placed(*operands):
        return run(
            *(
                pltpu.with_memory_space_constraint(x, pltpu.HBM) if i == "h" else x
                for i, x in zip(ins, operands, strict=True)
            )
        )

    return placed


def vmem(dims, dtype=F32):
    return jax.ShapeDtypeStruct(dims, dtype), "v"


def copies(sems, *pairs):
    started = [pltpu.make_async_copy(src, dst, sems.at[i]) for i, (src, dst) in enumerate(pairs)]
    for one in started:
        one.start()
    return started


def rows_of(parts, dtype):
    return jnp.concatenate([p.astype(F32) for p in parts], axis=0).astype(dtype)


def nt(left, right):
    return lax.dot_general(left, right, (((1,), (1,)), ((), ())), preferred_element_type=F32)


def nn(left, right):
    return jnp.dot(left, right, preferred_element_type=F32)


def prior(lengths, rank, blocks):
    total = jnp.int32(0)
    for i in range(blocks):
        total = total + jnp.where(i < rank, lengths[i], 0)
    return total


def averager():
    row = lax.broadcasted_iota(jnp.int32, (PAIR, PAIR), 0)
    col = lax.broadcasted_iota(jnp.int32, (PAIR, PAIR), 1)
    return jnp.where((row < HEAD) == (col < HEAD), 1.0 / HEAD, 0.0).astype(BF16)


def head_norm(field, average, gain):
    rows, width = field.shape
    pairs = [field[:, at : at + PAIR].astype(F32) for at in range(0, width, PAIR)]
    tall = jnp.concatenate(pairs, axis=0)
    centre = tall - nn(tall.astype(BF16), average)
    square = centre * centre
    high = square.astype(BF16)
    low = (square - high.astype(F32)).astype(BF16)
    spread = nn(high, average) + nn(low, average)
    normed = centre * lax.rsqrt(spread + head_eps) * gain
    return [normed[rows * p : rows * p + rows] for p in range(len(pairs))]


def rope_tables(start, rows):
    lane = lax.broadcasted_iota(jnp.int32, (rows, PAIR), 1)
    pos = (lax.broadcasted_iota(jnp.int32, (rows, PAIR), 0) + start).astype(F32)
    frame = jnp.floor((pos + 0.5) * (1.0 / (HP * WP)))
    line = jnp.floor((pos + 0.5) * (1.0 / WP))
    across = pos - line * WP
    height = line - frame * HP
    pair = (lane % HEAD) // 2
    in_frame = pair < 8
    in_height = pair < 20
    coord = jnp.where(in_frame, frame, jnp.where(in_height, height, across))
    step = jnp.where(in_frame, pair, jnp.where(in_height, pair - 8, pair - 20)).astype(F32)
    rate = jnp.where(in_frame, 2.0 / 16, 2.0 / 24)
    angle = coord * jnp.exp(step * rate * (-math.log(10000.0)))
    sine = jnp.sin(angle)
    return jnp.cos(angle), jnp.where(lane % 2 == 0, -sine, sine)


def rotate(field, cos_table, sin_table):
    even = lax.broadcasted_iota(jnp.int32, field.shape, 1) % 2 == 0
    other = jnp.where(even, pltpu.roll(field, PAIR - 1, 1), pltpu.roll(field, 1, 1))
    return field * cos_table + other * sin_table


def twice(gain_ref):
    gain = gain_ref[...]
    return jnp.concatenate([gain, gain], axis=1)


def pack_keys_kernel(blocks, lengths_at, keys_at, values_at, gain_at, packed, lengths, keys, values, gain, sems):
    arriving = copies(sems, (lengths_at, lengths), (keys_at, keys), (gain_at, gain), (values_at, values))
    rows, width = keys.shape[1:]
    average = averager()
    arriving[0].wait()
    tables = rope_tables(prior(lengths, lax.axis_index("seq"), blocks), rows)
    arriving[1].wait()
    arriving[2].wait()
    wide = twice(gain)
    for p, normed in enumerate(head_norm(keys[0], average, wide)):
        packed[:, PAIR * p : PAIR * p + PAIR] = rotate(normed, *tables).astype(BF16)
    arriving[3].wait()
    packed[:, width:] = values[0]


def queries_kernel(
    blocks, order, lengths_at, queries_at, text_keys_at, q_gain_at, k_gain_at, text_values_at, weight_at,
    stacked, text_scores, bias, text_values, weight, lengths, queries, text_keys, q_gain, k_gain, sems,
):
    arriving = copies(
        sems, (lengths_at, lengths), (queries_at, queries), (q_gain_at, q_gain), (k_gain_at, k_gain),
        (text_keys_at, text_keys), (text_values_at, text_values), (weight_at, weight),
    )
    rows, width = queries.shape[1:]
    rank = lax.axis_index("seq")
    average = averager()
    left = lax.broadcasted_iota(jnp.int32, (rows, PAIR), 1) < HEAD
    lane = lax.broadcasted_iota(jnp.int32, bias.shape, 1)
    live = lane < 0
    arriving[0].wait()
    for i, block in enumerate(order(rank)):
        live = live | ((lane >= i * rows) & (lane < i * rows + lengths[block]))
    bias[...] = jnp.where(live, 0.0, -jnp.inf)
    tables = rope_tables(prior(lengths, rank, blocks), rows)
    for one in arriving[1:5]:
        one.wait()
    q_wide, k_wide = twice(q_gain), twice(k_gain)
    text_hat = []
    for at in range(0, width, PAIR):
        text_hat += head_norm(text_keys[0, :, at : at + PAIR], average, k_wide)
    for p, normed in enumerate(head_norm(queries[0], average, q_wide)):
        query = rotate(normed, *tables)
        query = query.astype(BF16).astype(F32) * 0.125
        both = jnp.concatenate([jnp.where(left, query, 0.0), jnp.where(left, 0.0, query)], axis=0)
        both = both.astype(BF16)
        stacked[p] = both
        text_scores[p] = nt(both, text_hat[p].astype(BF16))
    arriving[5].wait()
    arriving[6].wait()


def attend_kernel(n_blocks, sends, stacked, text_scores, bias, text_values, weight, *rest):
    gathered, attended, outs = rest[:n_blocks], rest[n_blocks], rest[n_blocks + 1 :]
    pairs, double = stacked.shape[:2]
    rows, width = double // 2, pairs * PAIR
    if n_blocks > 1:
        video = rows_of([g[...] for g in gathered], BF16)
    else:
        video = gathered[0][...]
    left = lax.broadcasted_iota(jnp.int32, (rows, PAIR), 1) < HEAD
    parts = []
    for p in range(pairs):
        at = p * PAIR
        scores_t = text_scores[p]
        scores_v = nt(stacked[p], video[:, at : at + PAIR]) + bias[...]
        row_max = jnp.maximum(
            jnp.max(scores_t, axis=1, keepdims=True), jnp.max(scores_v, axis=1, keepdims=True)
        )
        weights_t = jnp.exp(scores_t - row_max)
        weights_v = jnp.exp(scores_v - row_max)
        totals = jnp.sum(weights_t, axis=1, keepdims=True) + jnp.sum(weights_v, axis=1, keepdims=True)
        mixed = nn(weights_t.astype(BF16), text_values[0, :, at : at + PAIR])
        mixed = mixed + nn(weights_v.astype(BF16), video[:, width + at : width + at + PAIR])
        mixed = mixed / totals
        parts.append(jnp.where(left, mixed[:rows], mixed[rows:]).astype(BF16))
    joined = jnp.concatenate(parts, axis=1)
    attended[...] = joined
    project(sends, joined, weight, outs)


def project(sends, joined, weight, outs):
    for out, block in zip(outs, sends(lax.axis_index("tp"))):
        columns = out.shape[1]
        at = pl.multiple_of(block * columns, columns)
        out[...] = nn(joined, weight[:, pl.ds(at, columns)]).astype(out.dtype)


def project_kernel(sends, attended, weight, *outs):
    project(sends, attended[...], weight, outs)


def keep_kernel(value, out, sem):
    (one,) = copies(sem, (value, out.at[0]))
    one.wait()


def residual_kernel(
    tp, lengths, alphas, step, attended, weight, stream, gate, shift, scale, proj, latents,
    base, factor, split, consts, coefs,
):
    rank = lax.axis_index("tp")
    rows, columns = base.shape
    count = lengths[lax.axis_index("seq")]
    alive = lax.broadcasted_iota(jnp.int32, (rows, 1), 0) < count
    factor[...] = jnp.where(alive, gate[...], 0.0)
    channels = proj.shape[0]
    plain = proj[...]
    scaled = plain * (1.0 + scale[...])
    high = scaled.astype(BF16)
    rest = scaled - high.astype(F32)
    middle = rest.astype(BF16)
    split[0:channels] = high
    split[channels : 2 * channels] = middle
    split[2 * channels : 3 * channels] = (rest - middle.astype(F32)).astype(BF16)
    split[3 * channels :] = jnp.ones((16, columns), BF16)
    lane = lax.broadcasted_iota(jnp.int32, consts.shape, 1)
    consts[...] = jnp.where(
        lane == rows,
        jnp.sum(scaled, axis=1, keepdims=True),
        jnp.where(lane == rows + 1, jnp.sum(plain * shift[...], axis=1, keepdims=True), 0.0),
    )
    at = step[0]
    now = jnp.full((8, LANES), alphas[at], F32)
    earlier = jnp.full((8, LANES), alphas[at - STRIDE], F32)
    coefs[0:8] = jnp.sqrt(now)
    coefs[8:16] = jnp.sqrt(1.0 - now)
    coefs[16:24] = jnp.sqrt(earlier)
    coefs[24:32] = jnp.sqrt(1.0 - earlier)
    lane8 = lax.broadcasted_iota(jnp.int32, (8, LANES), 1)
    coefs[32:40] = jnp.where(lane8 < count, 1.0, 0.0)
    coefs[40:48] = jnp.concatenate([latents[...], jnp.zeros((8, LANES - rows), F32)], axis=1)
    own = nn(attended[...], weight[:, pl.ds(pl.multiple_of(rank * columns, columns), columns)])
    base[...] = jnp.where(alive, stream[0].astype(F32) + gate[...] * own, 0.0)


def hidden_kernel(tp, routes, base, factor, split, consts, *rest):
    arrived, (hidden, *outs), scratch = rest[: tp - 1], rest[tp - 1 : -1], rest[-1]
    summed = arrived[0][...].astype(F32)
    for block in arrived[1:]:
        summed = summed + block[...].astype(F32)
    value = (base[...] + factor[...] * summed).astype(BF16)
    hidden[...] = value
    rows = value.shape[0]
    channels = consts.shape[0]
    wide = value.astype(F32)
    square = wide * wide
    high = square.astype(BF16)
    low = (square - high.astype(F32)).astype(BF16)
    ones = split[3 * channels :]
    first = nt(split[...], value)
    partial = first[:channels] + first[channels : 2 * channels] + first[2 * channels : 3 * channels]
    total = first[3 * channels : 3 * channels + 8]
    squares = (nt(ones, high) + nt(ones, low))[:8]
    blank = jnp.zeros((channels, LANES - rows), F32)
    scratch[...] = jnp.concatenate([partial, blank], axis=1) + consts[...]
    row = lax.broadcasted_iota(jnp.int32, (8, rows), 0)
    stats = jnp.concatenate([jnp.where(row == 0, total, squares), blank[:8]], axis=1)
    rank = lax.axis_index("tp")
    for i, out in enumerate(outs):
        block = entry(routes[i], rank)
        for half in range(2):
            out[8 * half : 8 * half + 8] = scratch[pl.ds(pl.multiple_of((half * tp + block) * 8, 8), 8)]
        out[16:24] = stats


def total_kernel(own, *rest):
    arrived, (mine, other) = rest[:-2], rest[-2:]
    total = own[...]
    for block in arrived:
        total = total + block[...]
    half = lax.axis_index("cfg")
    first, second, stats = total[0:8], total[8:16], total[16:24]
    mine[0:8] = jnp.where(half == 0, first, second)
    mine[8:16] = stats
    other[0:8] = jnp.where(half == 0, second, first)
    other[8:16] = stats


def step_kernel(features, mine, theirs, coefs, out):
    rows = out.shape[1]

    def predict(block, consts):
        sums = block[0:8, :rows]
        mean = block[8:9, :rows] / features
        square = block[9:10, :rows] / features
        spread = lax.rsqrt(square - mean * mean + final_eps)
        return spread * (sums - mean * consts[0:8, rows : rows + 1]) + consts[0:8, rows + 1 : rows + 2]

    own, partner = predict(mine, mine), predict(theirs, mine)
    is_conditioned = lax.axis_index("cfg") == 0
    conditioned = jnp.where(is_conditioned, own, partner)
    unconditioned = jnp.where(is_conditioned, partner, own)
    guided = unconditioned + guide_scale * (conditioned - unconditioned)
    root_now, rest_now, root_next, rest_next, live, latents = (
        coefs[8 * i : 8 * i + 8, :rows] for i in range(6)
    )
    clean = root_now * latents - rest_now * guided
    noise = root_now * guided + rest_now * latents
    out[...] = jnp.where(live > 0.0, root_next * clean + rest_next * noise, 0.0)


def exchange(value, axis, distance):
    return lax.ppermute(value, axis, [(i, i ^ distance) for i in range(lax.axis_size(axis))])


def send(value, axis, route):
    return lax.ppermute(value, axis, list(enumerate(route)))


def entry(route, rank):
    place = jnp.int32(route[0])
    for i, to in enumerate(route[1:], 1):
        place = jnp.where(rank == i, to, place)
    return place


def shards(
    stream, queries, keys, values, text_keys, text_values, out_weight, gate, shift, scale, proj_weight,
    q_gain, k_gain, lengths, latents, alphas, step_index,
):
    blocks = lax.axis_size("seq")
    tp = lax.axis_size("tp")
    rows, width = queries.shape[1:]
    columns = stream.shape[2]
    text = text_keys.shape[1]
    channels = proj_weight.shape[1]
    pairs = width // PAIR
    direct = blocks <= 4 and blocks & (blocks - 1) == 0
    q_gain, k_gain = q_gain.reshape(1, HEAD), k_gain.reshape(1, HEAD)
    one_gain = pltpu.VMEM(q_gain.shape, F32)
    counts = pltpu.SMEM(lengths.shape, jnp.int32)

    (packed,) = call(
        functools.partial(pack_keys_kernel, blocks),
        [vmem((rows, 2 * width), BF16)],
        "hhhh",
        [counts, pltpu.VMEM(keys.shape, BF16), pltpu.VMEM(values.shape, BF16), one_gain, pltpu.SemaphoreType.DMA((4,))],
        cost=2000000,
    )(lengths, keys, values, k_gain)
    if direct:
        gathered = [packed] + [exchange(packed, "seq", d) for d in (3, 2, 1)]
        order = lambda rank: [rank] + [rank ^ d for d in (3, 2, 1)]
    else:
        gathered = [lax.all_gather(packed, "seq", axis=0, tiled=True)]
        order = lambda rank: range(blocks)
    stacked, text_scores, bias, held_values, held_weight = call(
        functools.partial(queries_kernel, blocks, order),
        [
            vmem((pairs, 2 * rows, PAIR), BF16),
            vmem((pairs, 2 * rows, text)),
            vmem((1, blocks * rows)),
            vmem(text_values.shape, BF16),
            vmem(out_weight.shape, BF16),
        ],
        "hhhhhhh",
        [
            counts, pltpu.VMEM(queries.shape, BF16), pltpu.VMEM(text_keys.shape, BF16), one_gain, one_gain,
            pltpu.SemaphoreType.DMA((7,)),
        ],
        cost=20000000,
    )(lengths, queries, text_keys, q_gain, k_gain, text_values, out_weight)
    routes = [[i ^ d for i in range(tp)] for d in [3, 2, 1]]
    late_routes = [[i ^ d for i in range(tp)] for d in (3, 2, 1)]
    attended, *outgoing = call(
        functools.partial(attend_kernel, len(gathered), lambda rank: [entry(r, rank) for r in routes[:3]]),
        [vmem((rows, width), BF16)] + [vmem((rows, columns), BF16)] * 3,
        "v" * (5 + len(gathered)),
        cost=100000000,
    )(stacked, text_scores, bias, held_values, held_weight, *gathered)
    arrived = [send(block, "tp", r) for r, block in zip(routes, outgoing)]
    base, factor, split, consts, coefs = call(
        functools.partial(residual_kernel, tp),
        [
            vmem((rows, columns)),
            vmem((rows, columns)),
            vmem((3 * channels + 16, columns), BF16),
            vmem((channels, LANES)),
            vmem((48, LANES)),
        ],
        "sss" + "v" * 8,
        cost=100000000,
    )(
        lengths, alphas, step_index, attended, held_weight, stream, gate.reshape(1, columns),
        shift.reshape(1, columns), scale.reshape(1, columns), proj_weight.T, latents.T,
    )
    hidden, *partials = call(
        functools.partial(hidden_kernel, tp, [list(range(tp))] + late_routes),
        [vmem((rows, columns), BF16)] + [vmem((24, LANES))] * tp,
        "v" * (4 + tp - 1),
        [pltpu.VMEM((channels, LANES), F32)],
        cost=20000000,
    )(base, factor, split, consts, *arrived)
    shares = [send(block, "tp", r) for r, block in zip(late_routes, partials[1:])]
    (hidden_out,) = call(
        keep_kernel, [(jax.ShapeDtypeStruct(stream.shape, BF16), "h")], "v", [pltpu.SemaphoreType.DMA((1,))], cost=2000000
    )(hidden)
    mine, other = call(total_kernel, [vmem((16, LANES))] * 2, "v" * tp)(partials[0], *shares)
    theirs = exchange(other, "cfg", 1)
    (latents_out,) = call(
        functools.partial(step_kernel, columns * tp), [vmem((latents.shape[1], rows))], "vvv"
    )(mine, theirs, coefs)
    return hidden_out, latents_out.T


def solution(mesh):
    return jax.shard_map(
        shards,
        mesh=mesh,
        in_specs=(
            P("cfg", "seq", "tp"),
            P("cfg", "seq", "tp"),
            P("cfg", "seq", "tp"),
            P("cfg", "seq", "tp"),
            P("cfg", None, "tp"),
            P("cfg", None, "tp"),
            P("tp", None),
            P("tp"),
            P("tp"),
            P("tp"),
            P("tp", None),
            P(),
            P(),
            P(),
            P("seq", ("cfg", "tp")),
            P(),
            P(),
        ),
        out_specs=(P("cfg", "seq", "tp"), P("seq", ("cfg", "tp"))),
        check_vma=False,
    )
```

```python
import functools
import math

import jax
import jax.numpy as jnp
from jax import lax
from jax.experimental import pallas as pl
from jax.experimental.pallas import tpu as pltpu
from jax.sharding import PartitionSpec as P

HEAD = 64
PAIR = 2 * HEAD
HP = 30
WP = 45
STRIDE = 20
LANES = 128

guide_scale = 6.0
head_eps = 1e-06
final_eps = 1e-05

F32 = jnp.float32
BF16 = jnp.bfloat16
CROSS = (False, True)
VMEM_LIMIT = 24 * 1024 * 1024


def call(kernel, outs, ins, scratch=(), cost=0):
    spaces = {"v": pltpu.VMEM, "s": pltpu.SMEM, "h": pltpu.HBM}
    run = pl.pallas_call(
        kernel,
        out_shape=[o[0] for o in outs],
        in_specs=[pl.BlockSpec(memory_space=spaces[i]) for i in ins],
        out_specs=[pl.BlockSpec(memory_space=spaces[o[1]]) for o in outs],
        scratch_shapes=list(scratch),
        compiler_params=pltpu.CompilerParams(vmem_limit_bytes=VMEM_LIMIT),
        cost_estimate=pl.CostEstimate(flops=cost, bytes_accessed=cost // 64, transcendentals=0),
    )

    def placed(*operands):
        return run(
            *(
                pltpu.with_memory_space_constraint(x, pltpu.HBM) if i == "h" else x
                for i, x in zip(ins, operands, strict=True)
            )
        )

    return placed


def vmem(dims, dtype=F32):
    return jax.ShapeDtypeStruct(dims, dtype), "v"


def copies(sems, *pairs):
    started = [pltpu.make_async_copy(src, dst, sems.at[i]) for i, (src, dst) in enumerate(pairs)]
    for one in started:
        one.start()
    return started


def rows_of(parts, dtype):
    return jnp.concatenate([p.astype(F32) for p in parts], axis=0).astype(dtype)


def nt(left, right):
    return lax.dot_general(left, right, (((1,), (1,)), ((), ())), preferred_element_type=F32)


def nn(left, right):
    return jnp.dot(left, right, preferred_element_type=F32)


def prior(lengths, rank, blocks):
    total = jnp.int32(0)
    for i in range(blocks):
        total = total + jnp.where(i < rank, lengths[i], 0)
    return total


def averager():
    row = lax.broadcasted_iota(jnp.int32, (PAIR, PAIR), 0)
    col = lax.broadcasted_iota(jnp.int32, (PAIR, PAIR), 1)
    return jnp.where((row < HEAD) == (col < HEAD), 1.0 / HEAD, 0.0).astype(BF16)


def head_norm(field, average, gain):
    rows, width = field.shape
    pairs = [field[:, at : at + PAIR].astype(F32) for at in range(0, width, PAIR)]
    tall = jnp.concatenate(pairs, axis=0)
    centre = tall - nn(tall.astype(BF16), average)
    square = centre * centre
    high = square.astype(BF16)
    low = (square - high.astype(F32)).astype(BF16)
    spread = nn(high, average) + nn(low, average)
    normed = centre * lax.rsqrt(spread + head_eps) * gain
    return [normed[rows * p : rows * p + rows] for p in range(len(pairs))]


def rope_tables(start, rows):
    lane = lax.broadcasted_iota(jnp.int32, (rows, PAIR), 1)
    pos = (lax.broadcasted_iota(jnp.int32, (rows, PAIR), 0) + start).astype(F32)
    frame = jnp.floor((pos + 0.5) * (1.0 / (HP * WP)))
    line = jnp.floor((pos + 0.5) * (1.0 / WP))
    across = pos - line * WP
    height = line - frame * HP
    pair = (lane % HEAD) // 2
    in_frame = pair < 8
    in_height = pair < 20
    coord = jnp.where(in_frame, frame, jnp.where(in_height, height, across))
    step = jnp.where(in_frame, pair, jnp.where(in_height, pair - 8, pair - 20)).astype(F32)
    rate = jnp.where(in_frame, 2.0 / 16, 2.0 / 24)
    angle = coord * jnp.exp(step * rate * (-math.log(10000.0)))
    sine = jnp.sin(angle)
    return jnp.cos(angle), jnp.where(lane % 2 == 0, -sine, sine)


def rotate(field, cos_table, sin_table):
    even = lax.broadcasted_iota(jnp.int32, field.shape, 1) % 2 == 0
    other = jnp.where(even, pltpu.roll(field, PAIR - 1, 1), pltpu.roll(field, 1, 1))
    return field * cos_table + other * sin_table


def twice(gain_ref):
    gain = gain_ref[...]
    return jnp.concatenate([gain, gain], axis=1)


def pack_keys_kernel(blocks, lengths_at, keys_at, values_at, gain_at, packed, lengths, keys, values, gain, sems):
    arriving = copies(sems, (lengths_at, lengths), (keys_at, keys), (gain_at, gain), (values_at, values))
    rows, width = keys.shape[1:]
    average = averager()
    arriving[0].wait()
    tables = rope_tables(prior(lengths, lax.axis_index("seq"), blocks), rows)
    arriving[1].wait()
    arriving[2].wait()
    wide = twice(gain)
    for p, normed in enumerate(head_norm(keys[0], average, wide)):
        packed[:, PAIR * p : PAIR * p + PAIR] = rotate(normed, *tables).astype(BF16)
    arriving[3].wait()
    packed[:, width:] = values[0]


def queries_kernel(
    blocks, order, lengths_at, queries_at, text_keys_at, q_gain_at, k_gain_at, text_values_at, weight_at,
    stacked, text_scores, bias, text_values, weight, lengths, queries, text_keys, q_gain, k_gain, sems,
):
    arriving = copies(
        sems, (lengths_at, lengths), (queries_at, queries), (q_gain_at, q_gain), (k_gain_at, k_gain),
        (text_keys_at, text_keys), (text_values_at, text_values), (weight_at, weight),
    )
    rows, width = queries.shape[1:]
    rank = lax.axis_index("seq")
    average = averager()
    left = lax.broadcasted_iota(jnp.int32, (rows, PAIR), 1) < HEAD
    lane = lax.broadcasted_iota(jnp.int32, bias.shape, 1)
    live = lane < 0
    arriving[0].wait()
    for i, block in enumerate(order(rank)):
        live = live | ((lane >= i * rows) & (lane < i * rows + lengths[block]))
    bias[...] = jnp.where(live, 0.0, -jnp.inf)
    tables = rope_tables(prior(lengths, rank, blocks), rows)
    for one in arriving[1:5]:
        one.wait()
    q_wide, k_wide = twice(q_gain), twice(k_gain)
    text_hat = []
    for at in range(0, width, PAIR):
        text_hat += head_norm(text_keys[0, :, at : at + PAIR], average, k_wide)
    for p, normed in enumerate(head_norm(queries[0], average, q_wide)):
        query = rotate(normed, *tables)
        query = query.astype(BF16).astype(F32) * 0.125
        both = jnp.concatenate([jnp.where(left, query, 0.0), jnp.where(left, 0.0, query)], axis=0)
        both = both.astype(BF16)
        stacked[p] = both
        text_scores[p] = nt(both, text_hat[p].astype(BF16))
    arriving[5].wait()
    arriving[6].wait()


def attend_kernel(n_blocks, sends, stacked, text_scores, bias, text_values, weight, *rest):
    gathered, attended, outs = rest[:n_blocks], rest[n_blocks], rest[n_blocks + 1 :]
    pairs, double = stacked.shape[:2]
    rows, width = double // 2, pairs * PAIR
    if n_blocks > 1:
        video = rows_of([g[...] for g in gathered], BF16)
    else:
        video = gathered[0][...]
    left = lax.broadcasted_iota(jnp.int32, (rows, PAIR), 1) < HEAD
    parts = []
    for p in range(pairs):
        at = p * PAIR
        scores_t = text_scores[p]
        scores_v = nt(stacked[p], video[:, at : at + PAIR]) + bias[...]
        row_max = jnp.maximum(
            jnp.max(scores_t, axis=1, keepdims=True), jnp.max(scores_v, axis=1, keepdims=True)
        )
        weights_t = jnp.exp(scores_t - row_max)
        weights_v = jnp.exp(scores_v - row_max)
        totals = jnp.sum(weights_t, axis=1, keepdims=True) + jnp.sum(weights_v, axis=1, keepdims=True)
        mixed = nn(weights_t.astype(BF16), text_values[0, :, at : at + PAIR])
        mixed = mixed + nn(weights_v.astype(BF16), video[:, width + at : width + at + PAIR])
        mixed = mixed / totals
        parts.append(jnp.where(left, mixed[:rows], mixed[rows:]).astype(BF16))
    joined = jnp.concatenate(parts, axis=1)
    attended[...] = joined
    project(sends, joined, weight, outs)


def project(sends, joined, weight, outs):
    for out, block in zip(outs, sends(lax.axis_index("tp"))):
        columns = out.shape[1]
        at = pl.multiple_of(block * columns, columns)
        out[...] = nn(joined, weight[:, pl.ds(at, columns)]).astype(out.dtype)


def project_kernel(sends, attended, weight, *outs):
    project(sends, attended[...], weight, outs)


def keep_kernel(value, out, sem):
    (one,) = copies(sem, (value, out.at[0]))
    one.wait()


def residual_kernel(
    tp, lengths, alphas, step, attended, weight, stream, gate, shift, scale, proj, latents,
    base, factor, split, consts, coefs,
):
    rank = lax.axis_index("tp")
    rows, columns = base.shape
    count = lengths[lax.axis_index("seq")]
    alive = lax.broadcasted_iota(jnp.int32, (rows, 1), 0) < count
    factor[...] = jnp.where(alive, gate[...], 0.0)
    channels = proj.shape[0]
    plain = proj[...]
    scaled = plain * (1.0 + scale[...])
    high = scaled.astype(BF16)
    rest = scaled - high.astype(F32)
    middle = rest.astype(BF16)
    split[0:channels] = high
    split[channels : 2 * channels] = middle
    split[2 * channels : 3 * channels] = (rest - middle.astype(F32)).astype(BF16)
    split[3 * channels :] = jnp.ones((16, columns), BF16)
    lane = lax.broadcasted_iota(jnp.int32, consts.shape, 1)
    consts[...] = jnp.where(
        lane == rows,
        jnp.sum(scaled, axis=1, keepdims=True),
        jnp.where(lane == rows + 1, jnp.sum(plain * shift[...], axis=1, keepdims=True), 0.0),
    )
    at = step[0]
    now = jnp.full((8, LANES), alphas[at], F32)
    earlier = jnp.full((8, LANES), alphas[at - STRIDE], F32)
    coefs[0:8] = jnp.sqrt(now)
    coefs[8:16] = jnp.sqrt(1.0 - now)
    coefs[16:24] = jnp.sqrt(earlier)
    coefs[24:32] = jnp.sqrt(1.0 - earlier)
    lane8 = lax.broadcasted_iota(jnp.int32, (8, LANES), 1)
    coefs[32:40] = jnp.where(lane8 < count, 1.0, 0.0)
    coefs[40:48] = jnp.concatenate([latents[...], jnp.zeros((8, LANES - rows), F32)], axis=1)
    own = nn(attended[...], weight[:, pl.ds(pl.multiple_of(rank * columns, columns), columns)])
    base[...] = jnp.where(alive, stream[0].astype(F32) + gate[...] * own, 0.0)


def hidden_kernel(tp, routes, base, factor, split, consts, *rest):
    arrived, (hidden, *outs), scratch = rest[: tp - 1], rest[tp - 1 : -1], rest[-1]
    summed = arrived[0][...].astype(F32)
    for block in arrived[1:]:
        summed = summed + block[...].astype(F32)
    value = (base[...] + factor[...] * summed).astype(BF16)
    hidden[...] = value
    rows = value.shape[0]
    channels = consts.shape[0]
    wide = value.astype(F32)
    square = wide * wide
    high = square.astype(BF16)
    low = (square - high.astype(F32)).astype(BF16)
    ones = split[3 * channels :]
    first = nt(split[...], value)
    partial = first[:channels] + first[channels : 2 * channels] + first[2 * channels : 3 * channels]
    total = first[3 * channels : 3 * channels + 8]
    squares = (nt(ones, high) + nt(ones, low))[:8]
    blank = jnp.zeros((channels, LANES - rows), F32)
    scratch[...] = jnp.concatenate([partial, blank], axis=1) + consts[...]
    row = lax.broadcasted_iota(jnp.int32, (8, rows), 0)
    stats = jnp.concatenate([jnp.where(row == 0, total, squares), blank[:8]], axis=1)
    rank = lax.axis_index("tp")
    for i, out in enumerate(outs):
        block = entry(routes[i], rank)
        for half in range(2):
            out[8 * half : 8 * half + 8] = scratch[pl.ds(pl.multiple_of((half * tp + block) * 8, 8), 8)]
        out[16:24] = stats


def total_kernel(crossing, own, *rest):
    arrived, (mine, other) = rest[:-2], rest[-2:]
    totals = [own[...], jnp.zeros(own.shape, F32)]
    for cross, block in zip(crossing, arrived):
        totals[cross] = totals[cross] + block[...]
    first = lax.axis_index("cfg") == 0
    for i, total in enumerate(totals):
        low, high, stats = total[0:8], total[8:16], total[16:24]
        at = 16 * i
        mine[at : at + 8] = jnp.where(first, low, high)
        other[at : at + 8] = jnp.where(first, high, low)
        mine[at + 8 : at + 16] = stats
        other[at + 8 : at + 16] = stats


def step_kernel(features, mine, theirs, coefs, out):
    rows = out.shape[1]
    consts = mine[0:8, rows : rows + 2] + mine[16:24, rows : rows + 2]

    def predict(block):
        sums = block[0:8, :rows]
        mean = block[8:9, :rows] / features
        square = block[9:10, :rows] / features
        spread = lax.rsqrt(square - mean * mean + final_eps)
        return spread * (sums - mean * consts[:, 0:1]) + consts[:, 1:2]

    own, partner = predict(mine[0:16] + theirs[16:32]), predict(mine[16:32] + theirs[0:16])
    is_conditioned = lax.axis_index("cfg") == 0
    conditioned = jnp.where(is_conditioned, own, partner)
    unconditioned = jnp.where(is_conditioned, partner, own)
    guided = unconditioned + guide_scale * (conditioned - unconditioned)
    root_now, rest_now, root_next, rest_next, live, latents = (
        coefs[8 * i : 8 * i + 8, :rows] for i in range(6)
    )
    clean = root_now * latents - rest_now * guided
    noise = root_now * guided + rest_now * latents
    out[...] = jnp.where(live > 0.0, root_next * clean + rest_next * noise, 0.0)


def exchange(value, axis, distance):
    return lax.ppermute(value, axis, [(i, i ^ distance) for i in range(lax.axis_size(axis))])


def send(value, route, cross=False):
    if not cross:
        return lax.ppermute(value, "tp", list(enumerate(route)))
    tp = len(route)
    pairs = [(half * tp + i, (1 - half) * tp + to) for half in range(2) for i, to in enumerate(route)]
    return lax.ppermute(value, ("cfg", "tp"), pairs)


def entry(route, rank):
    place = jnp.int32(route[0])
    for i, to in enumerate(route[1:], 1):
        place = jnp.where(rank == i, to, place)
    return place


def shards(
    stream, queries, keys, values, text_keys, text_values, out_weight, gate, shift, scale, proj_weight,
    q_gain, k_gain, lengths, latents, alphas, step_index,
):
    blocks = lax.axis_size("seq")
    tp = lax.axis_size("tp")
    rows, width = queries.shape[1:]
    columns = stream.shape[2]
    text = text_keys.shape[1]
    channels = proj_weight.shape[1]
    pairs = width // PAIR
    direct = blocks <= 4 and blocks & (blocks - 1) == 0
    q_gain, k_gain = q_gain.reshape(1, HEAD), k_gain.reshape(1, HEAD)
    one_gain = pltpu.VMEM(q_gain.shape, F32)
    counts = pltpu.SMEM(lengths.shape, jnp.int32)

    (packed,) = call(
        functools.partial(pack_keys_kernel, blocks),
        [vmem((rows, 2 * width), BF16)],
        "hhhh",
        [counts, pltpu.VMEM(keys.shape, BF16), pltpu.VMEM(values.shape, BF16), one_gain, pltpu.SemaphoreType.DMA((4,))],
        cost=2000000,
    )(lengths, keys, values, k_gain)
    if direct:
        gathered = [packed] + [exchange(packed, "seq", d) for d in range(blocks - 1, 0, -1)]
        order = lambda rank: [rank] + [rank ^ d for d in range(blocks - 1, 0, -1)]
    else:
        gathered = [lax.all_gather(packed, "seq", axis=0, tiled=True)]
        order = lambda rank: range(blocks)
    stacked, text_scores, bias, held_values, held_weight = call(
        functools.partial(queries_kernel, blocks, order),
        [
            vmem((pairs, 2 * rows, PAIR), BF16),
            vmem((pairs, 2 * rows, text)),
            vmem((1, blocks * rows)),
            vmem(text_values.shape, BF16),
            vmem(out_weight.shape, BF16),
        ],
        "hhhhhhh",
        [
            counts, pltpu.VMEM(queries.shape, BF16), pltpu.VMEM(text_keys.shape, BF16), one_gain, one_gain,
            pltpu.SemaphoreType.DMA((7,)),
        ],
        cost=20000000,
    )(lengths, queries, text_keys, q_gain, k_gain, text_values, out_weight)
    distances = range(tp - 1, 0, -1)
    routes = [[i ^ d for i in range(tp)] for d in distances]
    crossing = [CROSS[d % 2] for d in distances]
    attended, *outgoing = call(
        functools.partial(attend_kernel, len(gathered), lambda rank: [entry(r, rank) for r in routes]),
        [vmem((rows, width), BF16)] + [vmem((rows, columns), BF16)] * (tp - 1),
        "v" * (5 + len(gathered)),
        cost=100000000,
    )(stacked, text_scores, bias, held_values, held_weight, *gathered)
    arrived = [send(block, r) for r, block in zip(routes, outgoing)]
    base, factor, split, consts, coefs = call(
        functools.partial(residual_kernel, tp),
        [
            vmem((rows, columns)),
            vmem((rows, columns)),
            vmem((3 * channels + 16, columns), BF16),
            vmem((channels, LANES)),
            vmem((48, LANES)),
        ],
        "sss" + "v" * 8,
        cost=100000000,
    )(
        lengths, alphas, step_index, attended, held_weight, stream, gate.reshape(1, columns),
        shift.reshape(1, columns), scale.reshape(1, columns), proj_weight.T, latents.T,
    )
    hidden, *partials = call(
        functools.partial(hidden_kernel, tp, [list(range(tp))] + routes),
        [vmem((rows, columns), BF16)] + [vmem((24, LANES))] * tp,
        "v" * (4 + tp - 1),
        [pltpu.VMEM((channels, LANES), F32)],
        cost=20000000,
    )(base, factor, split, consts, *arrived)
    shares = [send(block, r, cross) for r, cross, block in zip(routes, crossing, partials[1:])]
    (hidden_out,) = call(
        keep_kernel, [(jax.ShapeDtypeStruct(stream.shape, BF16), "h")], "v", [pltpu.SemaphoreType.DMA((1,))], cost=2000000
    )(hidden)
    mine, other = call(functools.partial(total_kernel, crossing), [vmem((32, LANES))] * 2, "v" * tp)(partials[0], *shares)
    theirs = exchange(other, "cfg", 1)
    (latents_out,) = call(
        functools.partial(step_kernel, columns * tp), [vmem((latents.shape[1], rows))], "vvv"
    )(mine, theirs, coefs)
    return hidden_out, latents_out.T


def solution(mesh):
    return jax.shard_map(
        shards,
        mesh=mesh,
        in_specs=(
            P("cfg", "seq", "tp"),
            P("cfg", "seq", "tp"),
            P("cfg", "seq", "tp"),
            P("cfg", "seq", "tp"),
            P("cfg", None, "tp"),
            P("cfg", None, "tp"),
            P("tp", None),
            P("tp"),
            P("tp"),
            P("tp"),
            P("tp", None),
            P(),
            P(),
            P(),
            P("seq", ("cfg", "tp")),
            P(),
            P(),
        ),
        out_specs=(P("cfg", "seq", "tp"), P("seq", ("cfg", "tp"))),
        check_vma=False,
    )
```

```python
import functools
import math

import jax
import jax.numpy as jnp
from jax import lax
from jax.experimental import pallas as pl
from jax.experimental.pallas import tpu as pltpu
from jax.sharding import PartitionSpec as P

HEAD = 64
PAIR = 2 * HEAD
HP = 30
WP = 45
STRIDE = 20
LANES = 128

guide_scale = 6.0
head_eps = 1e-06
final_eps = 1e-05

F32 = jnp.float32
BF16 = jnp.bfloat16
CROSS = (False, True)
VMEM_LIMIT = 24 * 1024 * 1024


def call(kernel, outs, ins, scratch=(), cost=0):
    spaces = {"v": pltpu.VMEM, "s": pltpu.SMEM, "h": pltpu.HBM}
    run = pl.pallas_call(
        kernel,
        out_shape=[o[0] for o in outs],
        in_specs=[pl.BlockSpec(memory_space=spaces[i]) for i in ins],
        out_specs=[pl.BlockSpec(memory_space=spaces[o[1]]) for o in outs],
        scratch_shapes=list(scratch),
        compiler_params=pltpu.CompilerParams(vmem_limit_bytes=VMEM_LIMIT),
        cost_estimate=pl.CostEstimate(flops=cost, bytes_accessed=cost // 64, transcendentals=0),
    )

    def placed(*operands):
        return run(
            *(
                pltpu.with_memory_space_constraint(x, pltpu.HBM) if i == "h" else x
                for i, x in zip(ins, operands, strict=True)
            )
        )

    return placed


def vmem(dims, dtype=F32):
    return jax.ShapeDtypeStruct(dims, dtype), "v"


def copies(sems, *pairs):
    started = [pltpu.make_async_copy(src, dst, sems.at[i]) for i, (src, dst) in enumerate(pairs)]
    for one in started:
        one.start()
    return started


def rows_of(parts, dtype):
    return jnp.concatenate([p.astype(F32) for p in parts], axis=0).astype(dtype)


def nt(left, right):
    return lax.dot_general(left, right, (((1,), (1,)), ((), ())), preferred_element_type=F32)


def nn(left, right):
    return jnp.dot(left, right, preferred_element_type=F32)


def prior(lengths, rank, blocks):
    total = jnp.int32(0)
    for i in range(blocks):
        total = total + jnp.where(i < rank, lengths[i], 0)
    return total


def averager():
    row = lax.broadcasted_iota(jnp.int32, (PAIR, PAIR), 0)
    col = lax.broadcasted_iota(jnp.int32, (PAIR, PAIR), 1)
    return jnp.where((row < HEAD) == (col < HEAD), 1.0 / HEAD, 0.0).astype(BF16)


def head_norm(field, average, gain):
    rows, width = field.shape
    pairs = [field[:, at : at + PAIR].astype(F32) for at in range(0, width, PAIR)]
    tall = jnp.concatenate(pairs, axis=0)
    centre = tall - nn(tall.astype(BF16), average)
    square = centre * centre
    high = square.astype(BF16)
    low = (square - high.astype(F32)).astype(BF16)
    spread = nn(high, average) + nn(low, average)
    normed = centre * lax.rsqrt(spread + head_eps) * gain
    return [normed[rows * p : rows * p + rows] for p in range(len(pairs))]


def lane_norm(field, gain):
    rows, width = field.shape
    pairs = [field[:, at : at + PAIR].astype(F32) for at in range(0, width, PAIR)]
    tall = jnp.concatenate(pairs, axis=0)
    left = lax.broadcasted_iota(jnp.int32, tall.shape, 1) < HEAD

    def average(values):
        low = jnp.sum(jnp.where(left, values, 0.0), axis=1, keepdims=True)
        high = jnp.sum(jnp.where(left, 0.0, values), axis=1, keepdims=True)
        return jnp.where(left, low, high) * (1.0 / HEAD)

    centre = tall - average(tall)
    normed = centre * lax.rsqrt(average(centre * centre) + head_eps) * gain
    return [normed[rows * p : rows * p + rows] for p in range(len(pairs))]


def rope_tables(start, rows):
    lane = lax.broadcasted_iota(jnp.int32, (rows, PAIR), 1)
    pos = (lax.broadcasted_iota(jnp.int32, (rows, PAIR), 0) + start).astype(F32)
    frame = jnp.floor((pos + 0.5) * (1.0 / (HP * WP)))
    line = jnp.floor((pos + 0.5) * (1.0 / WP))
    across = pos - line * WP
    height = line - frame * HP
    pair = (lane % HEAD) // 2
    in_frame = pair < 8
    in_height = pair < 20
    coord = jnp.where(in_frame, frame, jnp.where(in_height, height, across))
    step = jnp.where(in_frame, pair, jnp.where(in_height, pair - 8, pair - 20)).astype(F32)
    rate = jnp.where(in_frame, 2.0 / 16, 2.0 / 24)
    angle = coord * jnp.exp(step * rate * (-math.log(10000.0)))
    sine = jnp.sin(angle)
    return jnp.cos(angle), jnp.where(lane % 2 == 0, -sine, sine)


def rotate(field, cos_table, sin_table):
    even = lax.broadcasted_iota(jnp.int32, field.shape, 1) % 2 == 0
    other = jnp.where(even, pltpu.roll(field, PAIR - 1, 1), pltpu.roll(field, 1, 1))
    return field * cos_table + other * sin_table


def twice(gain_ref):
    gain = gain_ref[...]
    return jnp.concatenate([gain, gain], axis=1)


def pack_keys_kernel(blocks, lengths_at, keys_at, values_at, gain_at, packed, lengths, keys, values, gain, sems):
    arriving = copies(sems, (lengths_at, lengths), (keys_at, keys), (gain_at, gain), (values_at, values))
    rows, width = keys.shape[1:]
    arriving[0].wait()
    tables = rope_tables(prior(lengths, lax.axis_index("seq"), blocks), rows)
    arriving[1].wait()
    arriving[2].wait()
    wide = twice(gain)
    for p, normed in enumerate(lane_norm(keys[0], wide)):
        packed[:, PAIR * p : PAIR * p + PAIR] = rotate(normed, *tables).astype(BF16)
    arriving[3].wait()
    packed[:, width:] = values[0]


def queries_kernel(
    blocks, order, lengths_at, queries_at, text_keys_at, q_gain_at, k_gain_at, text_values_at, weight_at,
    stacked, text_scores, bias, text_values, weight, lengths, queries, text_keys, q_gain, k_gain, sems,
):
    arriving = copies(
        sems, (lengths_at, lengths), (queries_at, queries), (q_gain_at, q_gain), (k_gain_at, k_gain),
        (text_keys_at, text_keys), (text_values_at, text_values), (weight_at, weight),
    )
    rows, width = queries.shape[1:]
    rank = lax.axis_index("seq")
    average = averager()
    left = lax.broadcasted_iota(jnp.int32, (rows, PAIR), 1) < HEAD
    lane = lax.broadcasted_iota(jnp.int32, bias.shape, 1)
    live = lane < 0
    arriving[0].wait()
    for i, block in enumerate(order(rank)):
        live = live | ((lane >= i * rows) & (lane < i * rows + lengths[block]))
    bias[...] = jnp.where(live, 0.0, -jnp.inf)
    tables = rope_tables(prior(lengths, rank, blocks), rows)
    for one in arriving[1:5]:
        one.wait()
    q_wide, k_wide = twice(q_gain), twice(k_gain)
    text_hat = []
    for at in range(0, width, PAIR):
        text_hat += head_norm(text_keys[0, :, at : at + PAIR], average, k_wide)
    for p, normed in enumerate(head_norm(queries[0], average, q_wide)):
        query = rotate(normed, *tables)
        query = query.astype(BF16).astype(F32) * 0.125
        both = jnp.concatenate([jnp.where(left, query, 0.0), jnp.where(left, 0.0, query)], axis=0)
        both = both.astype(BF16)
        stacked[p] = both
        text_scores[p] = nt(both, text_hat[p].astype(BF16))
    arriving[5].wait()
    arriving[6].wait()


def attend_kernel(n_blocks, sends, stacked, text_scores, bias, text_values, weight, *rest):
    gathered, attended, outs = rest[:n_blocks], rest[n_blocks], rest[n_blocks + 1 :]
    pairs, double = stacked.shape[:2]
    rows, width = double // 2, pairs * PAIR
    if n_blocks > 1:
        video = rows_of([g[...] for g in gathered], BF16)
    else:
        video = gathered[0][...]
    left = lax.broadcasted_iota(jnp.int32, (rows, PAIR), 1) < HEAD
    parts = []
    for p in range(pairs):
        at = p * PAIR
        scores_t = text_scores[p]
        scores_v = nt(stacked[p], video[:, at : at + PAIR]) + bias[...]
        row_max = jnp.maximum(
            jnp.max(scores_t, axis=1, keepdims=True), jnp.max(scores_v, axis=1, keepdims=True)
        )
        weights_t = jnp.exp(scores_t - row_max)
        weights_v = jnp.exp(scores_v - row_max)
        totals = jnp.sum(weights_t, axis=1, keepdims=True) + jnp.sum(weights_v, axis=1, keepdims=True)
        mixed = nn(weights_t.astype(BF16), text_values[0, :, at : at + PAIR])
        mixed = mixed + nn(weights_v.astype(BF16), video[:, width + at : width + at + PAIR])
        mixed = mixed / totals
        parts.append(jnp.where(left, mixed[:rows], mixed[rows:]).astype(BF16))
    joined = jnp.concatenate(parts, axis=1)
    attended[...] = joined
    project(sends, joined, weight, outs)


def project(sends, joined, weight, outs):
    for out, block in zip(outs, sends(lax.axis_index("tp"))):
        columns = out.shape[1]
        at = pl.multiple_of(block * columns, columns)
        out[...] = nn(joined, weight[:, pl.ds(at, columns)]).astype(out.dtype)


def project_kernel(sends, attended, weight, *outs):
    project(sends, attended[...], weight, outs)


def keep_kernel(value, out, sem):
    (one,) = copies(sem, (value, out.at[0]))
    one.wait()


def residual_kernel(
    tp, lengths, alphas, step, attended, weight, stream, gate, shift, scale, proj, latents,
    base, factor, split, consts, coefs,
):
    rank = lax.axis_index("tp")
    rows, columns = base.shape
    count = lengths[lax.axis_index("seq")]
    alive = lax.broadcasted_iota(jnp.int32, (rows, 1), 0) < count
    factor[...] = jnp.where(alive, gate[...], 0.0)
    channels = proj.shape[0]
    plain = proj[...]
    scaled = plain * (1.0 + scale[...])
    high = scaled.astype(BF16)
    rest = scaled - high.astype(F32)
    middle = rest.astype(BF16)
    split[0:channels] = high
    split[channels : 2 * channels] = middle
    split[2 * channels : 3 * channels] = (rest - middle.astype(F32)).astype(BF16)
    split[3 * channels :] = jnp.ones((16, columns), BF16)
    lane = lax.broadcasted_iota(jnp.int32, consts.shape, 1)
    consts[...] = jnp.where(
        lane == rows,
        jnp.sum(scaled, axis=1, keepdims=True),
        jnp.where(lane == rows + 1, jnp.sum(plain * shift[...], axis=1, keepdims=True), 0.0),
    )
    at = step[0]
    now = jnp.full((8, LANES), alphas[at], F32)
    earlier = jnp.full((8, LANES), alphas[at - STRIDE], F32)
    coefs[0:8] = jnp.sqrt(now)
    coefs[8:16] = jnp.sqrt(1.0 - now)
    coefs[16:24] = jnp.sqrt(earlier)
    coefs[24:32] = jnp.sqrt(1.0 - earlier)
    lane8 = lax.broadcasted_iota(jnp.int32, (8, LANES), 1)
    coefs[32:40] = jnp.where(lane8 < count, 1.0, 0.0)
    coefs[40:48] = jnp.concatenate([latents[...], jnp.zeros((8, LANES - rows), F32)], axis=1)
    own = nn(attended[...], weight[:, pl.ds(pl.multiple_of(rank * columns, columns), columns)])
    base[...] = jnp.where(alive, stream[0].astype(F32) + gate[...] * own, 0.0)


def hidden_kernel(tp, routes, base, factor, split, consts, *rest):
    arrived, (hidden, *outs), scratch = rest[: tp - 1], rest[tp - 1 : -1], rest[-1]
    summed = arrived[0][...].astype(F32)
    for block in arrived[1:]:
        summed = summed + block[...].astype(F32)
    value = (base[...] + factor[...] * summed).astype(BF16)
    hidden[...] = value
    rows = value.shape[0]
    channels = consts.shape[0]
    wide = value.astype(F32)
    square = wide * wide
    high = square.astype(BF16)
    low = (square - high.astype(F32)).astype(BF16)
    ones = split[3 * channels :]
    first = nt(split[...], value)
    partial = first[:channels] + first[channels : 2 * channels] + first[2 * channels : 3 * channels]
    total = first[3 * channels : 3 * channels + 8]
    squares = (nt(ones, high) + nt(ones, low))[:8]
    blank = jnp.zeros((channels, LANES - rows), F32)
    scratch[...] = jnp.concatenate([partial, blank], axis=1) + consts[...]
    row = lax.broadcasted_iota(jnp.int32, (8, rows), 0)
    stats = jnp.concatenate([jnp.where(row == 0, total, squares), blank[:8]], axis=1)
    rank = lax.axis_index("tp")
    for i, out in enumerate(outs):
        block = entry(routes[i], rank)
        for half in range(2):
            out[8 * half : 8 * half + 8] = scratch[pl.ds(pl.multiple_of((half * tp + block) * 8, 8), 8)]
        out[16:24] = stats


def total_kernel(crossing, own, *rest):
    arrived, (mine, other) = rest[:-2], rest[-2:]
    totals = [own[...], jnp.zeros(own.shape, F32)]
    for cross, block in zip(crossing, arrived):
        totals[cross] = totals[cross] + block[...]
    first = lax.axis_index("cfg") == 0
    for i, total in enumerate(totals):
        low, high, stats = total[0:8], total[8:16], total[16:24]
        at = 16 * i
        mine[at : at + 8] = jnp.where(first, low, high)
        other[at : at + 8] = jnp.where(first, high, low)
        mine[at + 8 : at + 16] = stats
        other[at + 8 : at + 16] = stats


def step_kernel(features, mine, theirs, coefs, out):
    rows = out.shape[1]
    consts = mine[0:8, rows : rows + 2] + mine[16:24, rows : rows + 2]

    def predict(block):
        sums = block[0:8, :rows]
        mean = block[8:9, :rows] / features
        square = block[9:10, :rows] / features
        spread = lax.rsqrt(square - mean * mean + final_eps)
        return spread * (sums - mean * consts[:, 0:1]) + consts[:, 1:2]

    own, partner = predict(mine[0:16] + theirs[16:32]), predict(mine[16:32] + theirs[0:16])
    is_conditioned = lax.axis_index("cfg") == 0
    conditioned = jnp.where(is_conditioned, own, partner)
    unconditioned = jnp.where(is_conditioned, partner, own)
    guided = unconditioned + guide_scale * (conditioned - unconditioned)
    root_now, rest_now, root_next, rest_next, live, latents = (
        coefs[8 * i : 8 * i + 8, :rows] for i in range(6)
    )
    clean = root_now * latents - rest_now * guided
    noise = root_now * guided + rest_now * latents
    out[...] = jnp.where(live > 0.0, root_next * clean + rest_next * noise, 0.0)


def exchange(value, axis, distance):
    return lax.ppermute(value, axis, [(i, i ^ distance) for i in range(lax.axis_size(axis))])


def send(value, route, cross=False):
    if not cross:
        return lax.ppermute(value, "tp", list(enumerate(route)))
    tp = len(route)
    pairs = [(half * tp + i, (1 - half) * tp + to) for half in range(2) for i, to in enumerate(route)]
    return lax.ppermute(value, ("cfg", "tp"), pairs)


def entry(route, rank):
    place = jnp.int32(route[0])
    for i, to in enumerate(route[1:], 1):
        place = jnp.where(rank == i, to, place)
    return place


def shards(
    stream, queries, keys, values, text_keys, text_values, out_weight, gate, shift, scale, proj_weight,
    q_gain, k_gain, lengths, latents, alphas, step_index,
):
    blocks = lax.axis_size("seq")
    tp = lax.axis_size("tp")
    rows, width = queries.shape[1:]
    columns = stream.shape[2]
    text = text_keys.shape[1]
    channels = proj_weight.shape[1]
    pairs = width // PAIR
    direct = blocks <= 4 and blocks & (blocks - 1) == 0
    q_gain, k_gain = q_gain.reshape(1, HEAD), k_gain.reshape(1, HEAD)
    one_gain = pltpu.VMEM(q_gain.shape, F32)
    counts = pltpu.SMEM(lengths.shape, jnp.int32)

    (packed,) = call(
        functools.partial(pack_keys_kernel, blocks),
        [vmem((rows, 2 * width), BF16)],
        "hhhh",
        [counts, pltpu.VMEM(keys.shape, BF16), pltpu.VMEM(values.shape, BF16), one_gain, pltpu.SemaphoreType.DMA((4,))],
        cost=2000000,
    )(lengths, keys, values, k_gain)
    if direct:
        gathered = [packed] + [exchange(packed, "seq", d) for d in range(blocks - 1, 0, -1)]
        order = lambda rank: [rank] + [rank ^ d for d in range(blocks - 1, 0, -1)]
    else:
        gathered = [lax.all_gather(packed, "seq", axis=0, tiled=True)]
        order = lambda rank: range(blocks)
    stacked, text_scores, bias, held_values, held_weight = call(
        functools.partial(queries_kernel, blocks, order),
        [
            vmem((pairs, 2 * rows, PAIR), BF16),
            vmem((pairs, 2 * rows, text)),
            vmem((1, blocks * rows)),
            vmem(text_values.shape, BF16),
            vmem(out_weight.shape, BF16),
        ],
        "hhhhhhh",
        [
            counts, pltpu.VMEM(queries.shape, BF16), pltpu.VMEM(text_keys.shape, BF16), one_gain, one_gain,
            pltpu.SemaphoreType.DMA((7,)),
        ],
        cost=20000000,
    )(lengths, queries, text_keys, q_gain, k_gain, text_values, out_weight)
    distances = range(tp - 1, 0, -1)
    routes = [[i ^ d for i in range(tp)] for d in distances]
    crossing = [CROSS[d % 2] for d in distances]
    attended, *outgoing = call(
        functools.partial(attend_kernel, len(gathered), lambda rank: [entry(r, rank) for r in routes]),
        [vmem((rows, width), BF16)] + [vmem((rows, columns), BF16)] * (tp - 1),
        "v" * (5 + len(gathered)),
        cost=100000000,
    )(stacked, text_scores, bias, held_values, held_weight, *gathered)
    arrived = [send(block, r) for r, block in zip(routes, outgoing)]
    base, factor, split, consts, coefs = call(
        functools.partial(residual_kernel, tp),
        [
            vmem((rows, columns)),
            vmem((rows, columns)),
            vmem((3 * channels + 16, columns), BF16),
            vmem((channels, LANES)),
            vmem((48, LANES)),
        ],
        "sss" + "v" * 8,
        cost=100000000,
    )(
        lengths, alphas, step_index, attended, held_weight, stream, gate.reshape(1, columns),
        shift.reshape(1, columns), scale.reshape(1, columns), proj_weight.T, latents.T,
    )
    hidden, *partials = call(
        functools.partial(hidden_kernel, tp, [list(range(tp))] + routes),
        [vmem((rows, columns), BF16)] + [vmem((24, LANES))] * tp,
        "v" * (4 + tp - 1),
        [pltpu.VMEM((channels, LANES), F32)],
        cost=20000000,
    )(base, factor, split, consts, *arrived)
    shares = [send(block, r, cross) for r, cross, block in zip(routes, crossing, partials[1:])]
    (hidden_out,) = call(
        keep_kernel, [(jax.ShapeDtypeStruct(stream.shape, BF16), "h")], "v", [pltpu.SemaphoreType.DMA((1,))], cost=2000000
    )(hidden)
    mine, other = call(functools.partial(total_kernel, crossing), [vmem((32, LANES))] * 2, "v" * tp)(partials[0], *shares)
    theirs = exchange(other, "cfg", 1)
    (latents_out,) = call(
        functools.partial(step_kernel, columns * tp), [vmem((latents.shape[1], rows))], "vvv"
    )(mine, theirs, coefs)
    return hidden_out, latents_out.T


def solution(mesh):
    return jax.shard_map(
        shards,
        mesh=mesh,
        in_specs=(
            P("cfg", "seq", "tp"),
            P("cfg", "seq", "tp"),
            P("cfg", "seq", "tp"),
            P("cfg", "seq", "tp"),
            P("cfg", None, "tp"),
            P("cfg", None, "tp"),
            P("tp", None),
            P("tp"),
            P("tp"),
            P("tp"),
            P("tp", None),
            P(),
            P(),
            P(),
            P("seq", ("cfg", "tp")),
            P(),
            P(),
        ),
        out_specs=(P("cfg", "seq", "tp"), P("seq", ("cfg", "tp"))),
        check_vma=False,
    )
```

```python
import functools
import math

import jax
import jax.numpy as jnp
from jax import lax
from jax.experimental import pallas as pl
from jax.experimental.pallas import tpu as pltpu
from jax.sharding import PartitionSpec as P

HEAD = 64
PAIR = 2 * HEAD
HP = 30
WP = 45
STRIDE = 20
LANES = 128

guide_scale = 6.0
head_eps = 1e-06
final_eps = 1e-05

F32 = jnp.float32
BF16 = jnp.bfloat16
CROSS = (False, True)
VMEM_LIMIT = 24 * 1024 * 1024


def call(kernel, outs, ins, scratch=(), cost=0):
    spaces = {"v": pltpu.VMEM, "s": pltpu.SMEM, "h": pltpu.HBM}
    run = pl.pallas_call(
        kernel,
        out_shape=[o[0] for o in outs],
        in_specs=[pl.BlockSpec(memory_space=spaces[i]) for i in ins],
        out_specs=[pl.BlockSpec(memory_space=spaces[o[1]]) for o in outs],
        scratch_shapes=list(scratch),
        compiler_params=pltpu.CompilerParams(vmem_limit_bytes=VMEM_LIMIT),
        cost_estimate=pl.CostEstimate(flops=cost, bytes_accessed=cost // 64, transcendentals=0),
    )

    def placed(*operands):
        return run(
            *(
                pltpu.with_memory_space_constraint(x, pltpu.HBM) if i == "h" else x
                for i, x in zip(ins, operands, strict=True)
            )
        )

    return placed


def vmem(dims, dtype=F32):
    return jax.ShapeDtypeStruct(dims, dtype), "v"


def copies(sems, *pairs):
    started = [pltpu.make_async_copy(src, dst, sems.at[i]) for i, (src, dst) in enumerate(pairs)]
    for one in started:
        one.start()
    return started


def rows_of(parts, dtype):
    return jnp.concatenate([p.astype(F32) for p in parts], axis=0).astype(dtype)


def nt(left, right):
    return lax.dot_general(left, right, (((1,), (1,)), ((), ())), preferred_element_type=F32)


def nn(left, right):
    return jnp.dot(left, right, preferred_element_type=F32)


def prior(lengths, rank, blocks):
    total = jnp.int32(0)
    for i in range(blocks):
        total = total + jnp.where(i < rank, lengths[i], 0)
    return total


def averager():
    row = lax.broadcasted_iota(jnp.int32, (PAIR, PAIR), 0)
    col = lax.broadcasted_iota(jnp.int32, (PAIR, PAIR), 1)
    return jnp.where((row < HEAD) == (col < HEAD), 1.0 / HEAD, 0.0).astype(BF16)


def head_norm(field, average, gain):
    rows, width = field.shape
    pairs = [field[:, at : at + PAIR].astype(F32) for at in range(0, width, PAIR)]
    tall = jnp.concatenate(pairs, axis=0)
    centre = tall - nn(tall.astype(BF16), average)
    square = centre * centre
    high = square.astype(BF16)
    low = (square - high.astype(F32)).astype(BF16)
    spread = nn(high, average) + nn(low, average)
    normed = centre * lax.rsqrt(spread + head_eps) * gain
    return [normed[rows * p : rows * p + rows] for p in range(len(pairs))]


def lane_norm(field, gain):
    rows, width = field.shape
    pairs = [field[:, at : at + PAIR].astype(F32) for at in range(0, width, PAIR)]
    tall = jnp.concatenate(pairs, axis=0)
    left = lax.broadcasted_iota(jnp.int32, tall.shape, 1) < HEAD

    def average(values):
        low = jnp.sum(jnp.where(left, values, 0.0), axis=1, keepdims=True)
        high = jnp.sum(jnp.where(left, 0.0, values), axis=1, keepdims=True)
        return jnp.where(left, low, high) * (1.0 / HEAD)

    centre = tall - average(tall)
    normed = centre * lax.rsqrt(average(centre * centre) + head_eps) * gain
    return [normed[rows * p : rows * p + rows] for p in range(len(pairs))]


def rope_tables(start, rows):
    lane = lax.broadcasted_iota(jnp.int32, (rows, PAIR), 1)
    pos = (lax.broadcasted_iota(jnp.int32, (rows, PAIR), 0) + start).astype(F32)
    frame = jnp.floor((pos + 0.5) * (1.0 / (HP * WP)))
    line = jnp.floor((pos + 0.5) * (1.0 / WP))
    across = pos - line * WP
    height = line - frame * HP
    pair = (lane % HEAD) // 2
    in_frame = pair < 8
    in_height = pair < 20
    coord = jnp.where(in_frame, frame, jnp.where(in_height, height, across))
    step = jnp.where(in_frame, pair, jnp.where(in_height, pair - 8, pair - 20)).astype(F32)
    rate = jnp.where(in_frame, 2.0 / 16, 2.0 / 24)
    angle = coord * jnp.exp(step * rate * (-math.log(10000.0)))
    sine = jnp.sin(angle)
    return jnp.cos(angle), jnp.where(lane % 2 == 0, -sine, sine)


def rotate(field, cos_table, sin_table):
    even = lax.broadcasted_iota(jnp.int32, field.shape, 1) % 2 == 0
    other = jnp.where(even, pltpu.roll(field, PAIR - 1, 1), pltpu.roll(field, 1, 1))
    return field * cos_table + other * sin_table


def twice(gain_ref):
    gain = gain_ref[...]
    return jnp.concatenate([gain, gain], axis=1)


def pack_keys_kernel(blocks, lengths_at, keys_at, values_at, gain_at, packed, lengths, keys, values, gain, sems):
    arriving = copies(sems, (lengths_at, lengths), (keys_at, keys), (gain_at, gain), (values_at, values))
    rows, width = keys.shape[1:]
    arriving[0].wait()
    tables = rope_tables(prior(lengths, lax.axis_index("seq"), blocks), rows)
    arriving[1].wait()
    arriving[2].wait()
    wide = twice(gain)
    for p, normed in enumerate(lane_norm(keys[0], wide)):
        packed[:, PAIR * p : PAIR * p + PAIR] = rotate(normed, *tables).astype(BF16)
    arriving[3].wait()
    packed[:, width:] = values[0]


def queries_kernel(
    blocks, order, lengths_at, queries_at, text_keys_at, q_gain_at, k_gain_at, text_values_at, weight_at,
    stacked, text_scores, bias, text_values, weight, lengths, queries, text_keys, q_gain, k_gain, sems,
):
    arriving = copies(
        sems, (lengths_at, lengths), (queries_at, queries), (q_gain_at, q_gain), (k_gain_at, k_gain),
        (text_keys_at, text_keys), (text_values_at, text_values), (weight_at, weight),
    )
    rows, width = queries.shape[1:]
    rank = lax.axis_index("seq")
    average = averager()
    left = lax.broadcasted_iota(jnp.int32, (rows, PAIR), 1) < HEAD
    lane = lax.broadcasted_iota(jnp.int32, bias.shape, 1)
    live = lane < 0
    arriving[0].wait()
    for i, block in enumerate(order(rank)):
        live = live | ((lane >= i * rows) & (lane < i * rows + lengths[block]))
    bias[...] = jnp.where(live, 0.0, -jnp.inf)
    tables = rope_tables(prior(lengths, rank, blocks), rows)
    for one in arriving[1:5]:
        one.wait()
    q_wide, k_wide = twice(q_gain), twice(k_gain)
    text_hat = []
    for at in range(0, width, PAIR):
        text_hat += head_norm(text_keys[0, :, at : at + PAIR], average, k_wide)
    for p, normed in enumerate(head_norm(queries[0], average, q_wide)):
        query = rotate(normed, *tables)
        query = query.astype(BF16).astype(F32) * 0.125
        both = jnp.concatenate([jnp.where(left, query, 0.0), jnp.where(left, 0.0, query)], axis=0)
        both = both.astype(BF16)
        stacked[p] = both
        text_scores[p] = nt(both, text_hat[p].astype(BF16))
    arriving[5].wait()
    arriving[6].wait()


def attend_kernel(n_blocks, sends, stacked, text_scores, bias, text_values, weight, *rest):
    gathered, attended, outs = rest[:n_blocks], rest[n_blocks], rest[n_blocks + 1 :]
    pairs, double = stacked.shape[:2]
    rows, width = double // 2, pairs * PAIR
    if n_blocks > 1:
        video = rows_of([g[...] for g in gathered], BF16)
    else:
        video = gathered[0][...]
    left = lax.broadcasted_iota(jnp.int32, (rows, PAIR), 1) < HEAD
    parts = []
    for p in range(pairs):
        at = p * PAIR
        scores_t = text_scores[p]
        scores_v = nt(stacked[p], video[:, at : at + PAIR]) + bias[...]
        row_max = jnp.maximum(
            jnp.max(scores_t, axis=1, keepdims=True), jnp.max(scores_v, axis=1, keepdims=True)
        )
        weights_t = jnp.exp(scores_t - row_max)
        weights_v = jnp.exp(scores_v - row_max)
        totals = jnp.sum(weights_t, axis=1, keepdims=True) + jnp.sum(weights_v, axis=1, keepdims=True)
        mixed = nn(weights_t.astype(BF16), text_values[0, :, at : at + PAIR])
        mixed = mixed + nn(weights_v.astype(BF16), video[:, width + at : width + at + PAIR])
        mixed = mixed / totals
        parts.append(jnp.where(left, mixed[:rows], mixed[rows:]).astype(BF16))
    joined = jnp.concatenate(parts, axis=1)
    attended[...] = joined
    project(sends, joined, weight, outs)


def project(sends, joined, weight, outs):
    for out, block in zip(outs, sends(lax.axis_index("tp"))):
        columns = out.shape[1]
        at = pl.multiple_of(block * columns, columns)
        out[...] = nn(joined, weight[:, pl.ds(at, columns)]).astype(out.dtype)


def project_kernel(sends, attended, weight, *outs):
    project(sends, attended[...], weight, outs)


def keep_kernel(value, out, sem):
    (one,) = copies(sem, (value, out.at[0]))
    one.wait()


def residual_kernel(
    tp, lengths, alphas, step, attended, weight, stream, gate, shift, scale, proj, latents,
    base, factor, split, consts, coefs,
):
    rank = lax.axis_index("tp")
    rows, columns = base.shape
    count = lengths[lax.axis_index("seq")]
    alive = lax.broadcasted_iota(jnp.int32, (rows, 1), 0) < count
    factor[...] = jnp.where(alive, gate[...], 0.0)
    channels = proj.shape[0]
    plain = proj[...]
    scaled = plain * (1.0 + scale[...])
    high = scaled.astype(BF16)
    rest = scaled - high.astype(F32)
    middle = rest.astype(BF16)
    split[0:channels] = high
    split[channels : 2 * channels] = middle
    split[2 * channels : 3 * channels] = (rest - middle.astype(F32)).astype(BF16)
    split[3 * channels :] = jnp.ones((16, columns), BF16)
    lane = lax.broadcasted_iota(jnp.int32, consts.shape, 1)
    consts[...] = jnp.where(
        lane == rows,
        jnp.sum(scaled, axis=1, keepdims=True),
        jnp.where(lane == rows + 1, jnp.sum(plain * shift[...], axis=1, keepdims=True), 0.0),
    )
    at = step[0]
    now = jnp.full((8, LANES), alphas[at], F32)
    earlier = jnp.full((8, LANES), alphas[at - STRIDE], F32)
    root_now, rest_now = jnp.sqrt(now), jnp.sqrt(1.0 - now)
    root_next, rest_next = jnp.sqrt(earlier), jnp.sqrt(1.0 - earlier)
    lane8 = lax.broadcasted_iota(jnp.int32, (8, LANES), 1)
    noisy = jnp.concatenate([latents[...], jnp.zeros((8, LANES - rows), F32)], axis=1)
    coefs[0:8] = jnp.where(lane8 < count, (root_next * root_now + rest_next * rest_now) * noisy, 0.0)
    coefs[8:16] = jnp.where(lane8 < count, rest_next * root_now - root_next * rest_now, 0.0)
    own = nn(attended[...], weight[:, pl.ds(pl.multiple_of(rank * columns, columns), columns)])
    base[...] = jnp.where(alive, stream[0].astype(F32) + gate[...] * own, 0.0)


def hidden_kernel(tp, routes, base, factor, split, consts, *rest):
    arrived, (hidden, *outs), scratch = rest[: tp - 1], rest[tp - 1 : -1], rest[-1]
    summed = arrived[0][...].astype(F32)
    for block in arrived[1:]:
        summed = summed + block[...].astype(F32)
    value = (base[...] + factor[...] * summed).astype(BF16)
    hidden[...] = value
    rows = value.shape[0]
    channels = consts.shape[0]
    wide = value.astype(F32)
    square = wide * wide
    high = square.astype(BF16)
    low = (square - high.astype(F32)).astype(BF16)
    ones = split[3 * channels :]
    first = nt(split[...], value)
    partial = first[:channels] + first[channels : 2 * channels] + first[2 * channels : 3 * channels]
    total = first[3 * channels : 3 * channels + 8]
    squares = (nt(ones, high) + nt(ones, low))[:8]
    blank = jnp.zeros((channels, LANES - rows), F32)
    scratch[...] = jnp.concatenate([partial, blank], axis=1) + consts[...]
    row = lax.broadcasted_iota(jnp.int32, (8, rows), 0)
    stats = jnp.concatenate([jnp.where(row == 0, total, squares), blank[:8]], axis=1)
    rank = lax.axis_index("tp")
    for i, out in enumerate(outs):
        block = entry(routes[i], rank)
        for half in range(2):
            out[8 * half : 8 * half + 8] = scratch[pl.ds(pl.multiple_of((half * tp + block) * 8, 8), 8)]
        out[16:24] = stats


def total_kernel(crossing, own, *rest):
    arrived, (mine, other) = rest[:-2], rest[-2:]
    totals = [own[...], jnp.zeros(own.shape, F32)]
    for cross, block in zip(crossing, arrived):
        totals[cross] = totals[cross] + block[...]
    first = lax.axis_index("cfg") == 0
    for i, total in enumerate(totals):
        low, high, stats = total[0:8], total[8:16], total[16:24]
        at = 16 * i
        mine[at : at + 8] = jnp.where(first, low, high)
        other[at : at + 8] = jnp.where(first, high, low)
        mine[at + 8 : at + 16] = stats
        other[at + 8 : at + 16] = stats


def step_kernel(features, mine, theirs, coefs, out):
    rows = out.shape[1]
    consts = mine[0:8, rows : rows + 2] + mine[16:24, rows : rows + 2]

    def predict(block):
        sums = block[0:8, :rows]
        mean = block[8:9, :rows] / features
        square = block[9:10, :rows] / features
        spread = lax.rsqrt(square - mean * mean + final_eps)
        return spread * (sums - mean * consts[:, 0:1]) + consts[:, 1:2]

    own, partner = predict(mine[0:16] + theirs[16:32]), predict(mine[16:32] + theirs[0:16])
    is_conditioned = lax.axis_index("cfg") == 0
    conditioned = jnp.where(is_conditioned, own, partner)
    unconditioned = jnp.where(is_conditioned, partner, own)
    guided = unconditioned + guide_scale * (conditioned - unconditioned)
    out[...] = coefs[0:8, :rows] + coefs[8:16, :rows] * guided


def exchange(value, axis, distance):
    return lax.ppermute(value, axis, [(i, i ^ distance) for i in range(lax.axis_size(axis))])


def send(value, route, cross=False):
    if not cross:
        return lax.ppermute(value, "tp", list(enumerate(route)))
    tp = len(route)
    pairs = [(half * tp + i, (1 - half) * tp + to) for half in range(2) for i, to in enumerate(route)]
    return lax.ppermute(value, ("cfg", "tp"), pairs)


def entry(route, rank):
    place = jnp.int32(route[0])
    for i, to in enumerate(route[1:], 1):
        place = jnp.where(rank == i, to, place)
    return place


def shards(
    stream, queries, keys, values, text_keys, text_values, out_weight, gate, shift, scale, proj_weight,
    q_gain, k_gain, lengths, latents, alphas, step_index,
):
    blocks = lax.axis_size("seq")
    tp = lax.axis_size("tp")
    rows, width = queries.shape[1:]
    columns = stream.shape[2]
    text = text_keys.shape[1]
    channels = proj_weight.shape[1]
    pairs = width // PAIR
    direct = blocks <= 4 and blocks & (blocks - 1) == 0
    q_gain, k_gain = q_gain.reshape(1, HEAD), k_gain.reshape(1, HEAD)
    one_gain = pltpu.VMEM(q_gain.shape, F32)
    counts = pltpu.SMEM(lengths.shape, jnp.int32)

    (packed,) = call(
        functools.partial(pack_keys_kernel, blocks),
        [vmem((rows, 2 * width), BF16)],
        "hhhh",
        [counts, pltpu.VMEM(keys.shape, BF16), pltpu.VMEM(values.shape, BF16), one_gain, pltpu.SemaphoreType.DMA((4,))],
        cost=2000000,
    )(lengths, keys, values, k_gain)
    if direct:
        gathered = [packed] + [exchange(packed, "seq", d) for d in range(blocks - 1, 0, -1)]
        order = lambda rank: [rank] + [rank ^ d for d in range(blocks - 1, 0, -1)]
    else:
        gathered = [lax.all_gather(packed, "seq", axis=0, tiled=True)]
        order = lambda rank: range(blocks)
    stacked, text_scores, bias, held_values, held_weight = call(
        functools.partial(queries_kernel, blocks, order),
        [
            vmem((pairs, 2 * rows, PAIR), BF16),
            vmem((pairs, 2 * rows, text)),
            vmem((1, blocks * rows)),
            vmem(text_values.shape, BF16),
            vmem(out_weight.shape, BF16),
        ],
        "hhhhhhh",
        [
            counts, pltpu.VMEM(queries.shape, BF16), pltpu.VMEM(text_keys.shape, BF16), one_gain, one_gain,
            pltpu.SemaphoreType.DMA((7,)),
        ],
        cost=20000000,
    )(lengths, queries, text_keys, q_gain, k_gain, text_values, out_weight)
    distances = range(tp - 1, 0, -1)
    routes = [[i ^ d for i in range(tp)] for d in distances]
    crossing = [CROSS[d % 2] for d in distances]
    attended, *outgoing = call(
        functools.partial(attend_kernel, len(gathered), lambda rank: [entry(r, rank) for r in routes]),
        [vmem((rows, width), BF16)] + [vmem((rows, columns), BF16)] * (tp - 1),
        "v" * (5 + len(gathered)),
        cost=100000000,
    )(stacked, text_scores, bias, held_values, held_weight, *gathered)
    arrived = [send(block, r) for r, block in zip(routes, outgoing)]
    base, factor, split, consts, coefs = call(
        functools.partial(residual_kernel, tp),
        [
            vmem((rows, columns)),
            vmem((rows, columns)),
            vmem((3 * channels + 16, columns), BF16),
            vmem((channels, LANES)),
            vmem((16, LANES)),
        ],
        "sss" + "v" * 8,
        cost=100000000,
    )(
        lengths, alphas, step_index, attended, held_weight, stream, gate.reshape(1, columns),
        shift.reshape(1, columns), scale.reshape(1, columns), proj_weight.T, latents.T,
    )
    hidden, *partials = call(
        functools.partial(hidden_kernel, tp, [list(range(tp))] + routes),
        [vmem((rows, columns), BF16)] + [vmem((24, LANES))] * tp,
        "v" * (4 + tp - 1),
        [pltpu.VMEM((channels, LANES), F32)],
        cost=20000000,
    )(base, factor, split, consts, *arrived)
    shares = [send(block, r, cross) for r, cross, block in zip(routes, crossing, partials[1:])]
    (hidden_out,) = call(
        keep_kernel, [(jax.ShapeDtypeStruct(stream.shape, BF16), "h")], "v", [pltpu.SemaphoreType.DMA((1,))], cost=2000000
    )(hidden)
    mine, other = call(functools.partial(total_kernel, crossing), [vmem((32, LANES))] * 2, "v" * tp)(partials[0], *shares)
    theirs = exchange(other, "cfg", 1)
    (latents_out,) = call(
        functools.partial(step_kernel, columns * tp), [vmem((latents.shape[1], rows))], "vvv"
    )(mine, theirs, coefs)
    return hidden_out, latents_out.T


def solution(mesh):
    return jax.shard_map(
        shards,
        mesh=mesh,
        in_specs=(
            P("cfg", "seq", "tp"),
            P("cfg", "seq", "tp"),
            P("cfg", "seq", "tp"),
            P("cfg", "seq", "tp"),
            P("cfg", None, "tp"),
            P("cfg", None, "tp"),
            P("tp", None),
            P("tp"),
            P("tp"),
            P("tp"),
            P("tp", None),
            P(),
            P(),
            P(),
            P("seq", ("cfg", "tp")),
            P(),
            P(),
        ),
        out_specs=(P("cfg", "seq", "tp"), P("seq", ("cfg", "tp"))),
        check_vma=False,
    )
```

```python
import functools
import math

import jax
import jax.numpy as jnp
from jax import lax
from jax.experimental import pallas as pl
from jax.experimental.pallas import tpu as pltpu
from jax.sharding import PartitionSpec as P

HEAD = 64
PAIR = 2 * HEAD
HP = 30
WP = 45
STRIDE = 20
LANES = 128

guide_scale = 6.0
head_eps = 1e-06
final_eps = 1e-05

F32 = jnp.float32
BF16 = jnp.bfloat16
CROSS = (False, True)
VMEM_LIMIT = 24 * 1024 * 1024


def call(kernel, outs, ins, scratch=(), cost=0):
    spaces = {"v": pltpu.VMEM, "s": pltpu.SMEM, "h": pltpu.HBM}
    run = pl.pallas_call(
        kernel,
        out_shape=[o[0] for o in outs],
        in_specs=[pl.BlockSpec(memory_space=spaces[i]) for i in ins],
        out_specs=[pl.BlockSpec(memory_space=spaces[o[1]]) for o in outs],
        scratch_shapes=list(scratch),
        compiler_params=pltpu.CompilerParams(vmem_limit_bytes=VMEM_LIMIT),
        cost_estimate=pl.CostEstimate(flops=cost, bytes_accessed=cost // 64, transcendentals=0),
    )

    def placed(*operands):
        return run(
            *(
                pltpu.with_memory_space_constraint(x, pltpu.HBM) if i == "h" else x
                for i, x in zip(ins, operands, strict=True)
            )
        )

    return placed


def vmem(dims, dtype=F32):
    return jax.ShapeDtypeStruct(dims, dtype), "v"


def copies(sems, *pairs):
    started = [pltpu.make_async_copy(src, dst, sems.at[i]) for i, (src, dst) in enumerate(pairs)]
    for one in started:
        one.start()
    return started


def rows_of(parts, dtype):
    return jnp.concatenate([p.astype(F32) for p in parts], axis=0).astype(dtype)


def nt(left, right):
    return lax.dot_general(left, right, (((1,), (1,)), ((), ())), preferred_element_type=F32)


def nn(left, right):
    return jnp.dot(left, right, preferred_element_type=F32)


def prior(lengths, rank, blocks):
    total = jnp.int32(0)
    for i in range(blocks):
        total = total + jnp.where(i < rank, lengths[i], 0)
    return total


def averager():
    row = lax.broadcasted_iota(jnp.int32, (PAIR, PAIR), 0)
    col = lax.broadcasted_iota(jnp.int32, (PAIR, PAIR), 1)
    return jnp.where((row < HEAD) == (col < HEAD), 1.0 / HEAD, 0.0).astype(BF16)


def head_norm(field, average, gain):
    rows, width = field.shape
    pairs = [field[:, at : at + PAIR].astype(F32) for at in range(0, width, PAIR)]
    tall = jnp.concatenate(pairs, axis=0)
    centre = tall - nn(tall.astype(BF16), average)
    square = centre * centre
    high = square.astype(BF16)
    low = (square - high.astype(F32)).astype(BF16)
    spread = nn(high, average) + nn(low, average)
    normed = centre * lax.rsqrt(spread + head_eps) * gain
    return [normed[rows * p : rows * p + rows] for p in range(len(pairs))]


def lane_norm(field, gain):
    rows, width = field.shape
    pairs = [field[:, at : at + PAIR].astype(F32) for at in range(0, width, PAIR)]
    tall = jnp.concatenate(pairs, axis=0)
    left = lax.broadcasted_iota(jnp.int32, tall.shape, 1) < HEAD

    def average(values):
        low = jnp.sum(jnp.where(left, values, 0.0), axis=1, keepdims=True)
        high = jnp.sum(jnp.where(left, 0.0, values), axis=1, keepdims=True)
        return jnp.where(left, low, high) * (1.0 / HEAD)

    centre = tall - average(tall)
    normed = centre * lax.rsqrt(average(centre * centre) + head_eps) * gain
    return [normed[rows * p : rows * p + rows] for p in range(len(pairs))]


def rope_tables(start, rows):
    lane = lax.broadcasted_iota(jnp.int32, (rows, PAIR), 1)
    pos = (lax.broadcasted_iota(jnp.int32, (rows, PAIR), 0) + start).astype(F32)
    frame = jnp.floor((pos + 0.5) * (1.0 / (HP * WP)))
    line = jnp.floor((pos + 0.5) * (1.0 / WP))
    across = pos - line * WP
    height = line - frame * HP
    pair = (lane % HEAD) // 2
    in_frame = pair < 8
    in_height = pair < 20
    coord = jnp.where(in_frame, frame, jnp.where(in_height, height, across))
    step = jnp.where(in_frame, pair, jnp.where(in_height, pair - 8, pair - 20)).astype(F32)
    rate = jnp.where(in_frame, 2.0 / 16, 2.0 / 24)
    angle = coord * jnp.exp(step * rate * (-math.log(10000.0)))
    sine = jnp.sin(angle)
    return jnp.cos(angle), jnp.where(lane % 2 == 0, -sine, sine)


def rotate(field, cos_table, sin_table):
    even = lax.broadcasted_iota(jnp.int32, field.shape, 1) % 2 == 0
    other = jnp.where(even, pltpu.roll(field, PAIR - 1, 1), pltpu.roll(field, 1, 1))
    return field * cos_table + other * sin_table


def twice(gain_ref):
    gain = gain_ref[...]
    return jnp.concatenate([gain, gain], axis=1)


def pack_keys_kernel(blocks, lengths_at, keys_at, values_at, gain_at, packed, lengths, keys, values, gain, sems):
    arriving = copies(sems, (keys_at, keys), (lengths_at, lengths), (gain_at, gain), (values_at, values))
    rows, width = keys.shape[1:]
    for one in arriving[:3]:
        one.wait()
    tables = rope_tables(prior(lengths, lax.axis_index("seq"), blocks), rows)
    wide = twice(gain)
    for p, normed in enumerate(lane_norm(keys[0], wide)):
        packed[:, PAIR * p : PAIR * p + PAIR] = rotate(normed, *tables).astype(BF16)
    arriving[3].wait()
    packed[:, width:] = values[0]


def queries_kernel(
    blocks, order, lengths_at, queries_at, text_keys_at, q_gain_at, k_gain_at, text_values_at, weight_at,
    stacked, text_scores, bias, text_values, weight, lengths, queries, text_keys, q_gain, k_gain, sems,
):
    arriving = copies(
        sems, (lengths_at, lengths), (queries_at, queries), (q_gain_at, q_gain), (k_gain_at, k_gain),
        (text_keys_at, text_keys), (text_values_at, text_values), (weight_at, weight),
    )
    rows, width = queries.shape[1:]
    rank = lax.axis_index("seq")
    average = averager()
    left = lax.broadcasted_iota(jnp.int32, (rows, PAIR), 1) < HEAD
    lane = lax.broadcasted_iota(jnp.int32, bias.shape, 1)
    live = lane < 0
    arriving[0].wait()
    for i, block in enumerate(order(rank)):
        live = live | ((lane >= i * rows) & (lane < i * rows + lengths[block]))
    bias[...] = jnp.where(live, 0.0, -jnp.inf)
    tables = rope_tables(prior(lengths, rank, blocks), rows)
    for one in arriving[1:5]:
        one.wait()
    q_wide, k_wide = twice(q_gain), twice(k_gain)
    text_hat = []
    for at in range(0, width, PAIR):
        text_hat += head_norm(text_keys[0, :, at : at + PAIR], average, k_wide)
    for p, normed in enumerate(head_norm(queries[0], average, q_wide)):
        query = rotate(normed, *tables)
        query = query.astype(BF16).astype(F32) * 0.125
        both = jnp.concatenate([jnp.where(left, query, 0.0), jnp.where(left, 0.0, query)], axis=0)
        both = both.astype(BF16)
        stacked[p] = both
        text_scores[p] = nt(both, text_hat[p].astype(BF16))
    arriving[5].wait()
    arriving[6].wait()


def attend_kernel(n_blocks, sends, stacked, text_scores, bias, text_values, weight, *rest):
    gathered, attended, outs = rest[:n_blocks], rest[n_blocks], rest[n_blocks + 1 :]
    pairs, double = stacked.shape[:2]
    rows, width = double // 2, pairs * PAIR
    if n_blocks > 1:
        video = rows_of([g[...] for g in gathered], BF16)
    else:
        video = gathered[0][...]
    left = lax.broadcasted_iota(jnp.int32, (rows, PAIR), 1) < HEAD
    parts = []
    for p in range(pairs):
        at = p * PAIR
        scores_t = text_scores[p]
        scores_v = nt(stacked[p], video[:, at : at + PAIR]) + bias[...]
        row_max = jnp.maximum(
            jnp.max(scores_t, axis=1, keepdims=True), jnp.max(scores_v, axis=1, keepdims=True)
        )
        weights_t = jnp.exp(scores_t - row_max)
        weights_v = jnp.exp(scores_v - row_max)
        totals = jnp.sum(weights_t, axis=1, keepdims=True) + jnp.sum(weights_v, axis=1, keepdims=True)
        mixed = nn(weights_t.astype(BF16), text_values[0, :, at : at + PAIR])
        mixed = mixed + nn(weights_v.astype(BF16), video[:, width + at : width + at + PAIR])
        mixed = mixed / totals
        parts.append(jnp.where(left, mixed[:rows], mixed[rows:]).astype(BF16))
    joined = jnp.concatenate(parts, axis=1)
    attended[...] = joined
    project(sends, joined, weight, outs)


def project(sends, joined, weight, outs):
    for out, block in zip(outs, sends(lax.axis_index("tp"))):
        columns = out.shape[1]
        at = pl.multiple_of(block * columns, columns)
        out[...] = nn(joined, weight[:, pl.ds(at, columns)]).astype(out.dtype)


def project_kernel(sends, attended, weight, *outs):
    project(sends, attended[...], weight, outs)


def keep_kernel(value, out, sem):
    (one,) = copies(sem, (value, out.at[0]))
    one.wait()


def residual_kernel(
    tp, lengths, alphas, step, attended, weight, stream, gate, shift, scale, proj, latents,
    base, factor, split, consts, coefs,
):
    rank = lax.axis_index("tp")
    rows, columns = base.shape
    count = lengths[lax.axis_index("seq")]
    alive = lax.broadcasted_iota(jnp.int32, (rows, 1), 0) < count
    factor[...] = jnp.where(alive, gate[...], 0.0)
    channels = proj.shape[0]
    plain = proj[...]
    scaled = plain * (1.0 + scale[...])
    high = scaled.astype(BF16)
    rest = scaled - high.astype(F32)
    middle = rest.astype(BF16)
    split[0:channels] = high
    split[channels : 2 * channels] = middle
    split[2 * channels : 3 * channels] = (rest - middle.astype(F32)).astype(BF16)
    split[3 * channels :] = jnp.ones((16, columns), BF16)
    lane = lax.broadcasted_iota(jnp.int32, consts.shape, 1)
    consts[...] = jnp.where(
        lane == rows,
        jnp.sum(scaled, axis=1, keepdims=True),
        jnp.where(lane == rows + 1, jnp.sum(plain * shift[...], axis=1, keepdims=True), 0.0),
    )
    at = step[0]
    now = jnp.full((8, LANES), alphas[at], F32)
    earlier = jnp.full((8, LANES), alphas[at - STRIDE], F32)
    coefs[0:8] = jnp.sqrt(now)
    coefs[8:16] = jnp.sqrt(1.0 - now)
    coefs[16:24] = jnp.sqrt(earlier)
    coefs[24:32] = jnp.sqrt(1.0 - earlier)
    lane8 = lax.broadcasted_iota(jnp.int32, (8, LANES), 1)
    coefs[32:40] = jnp.where(lane8 < count, 1.0, 0.0)
    coefs[40:48] = jnp.concatenate([latents[...], jnp.zeros((8, LANES - rows), F32)], axis=1)
    own = nn(attended[...], weight[:, pl.ds(pl.multiple_of(rank * columns, columns), columns)])
    base[...] = jnp.where(alive, stream[0].astype(F32) + gate[...] * own, 0.0)


def hidden_kernel(tp, routes, base, factor, split, consts, *rest):
    arrived, (hidden, *outs), scratch = rest[: tp - 1], rest[tp - 1 : -1], rest[-1]
    summed = arrived[0][...].astype(F32)
    for block in arrived[1:]:
        summed = summed + block[...].astype(F32)
    value = (base[...] + factor[...] * summed).astype(BF16)
    hidden[...] = value
    rows = value.shape[0]
    channels = consts.shape[0]
    wide = value.astype(F32)
    square = wide * wide
    high = square.astype(BF16)
    low = (square - high.astype(F32)).astype(BF16)
    ones = split[3 * channels :]
    first = nt(split[...], value)
    partial = first[:channels] + first[channels : 2 * channels] + first[2 * channels : 3 * channels]
    total = first[3 * channels : 3 * channels + 8]
    squares = (nt(ones, high) + nt(ones, low))[:8]
    blank = jnp.zeros((channels, LANES - rows), F32)
    scratch[...] = jnp.concatenate([partial, blank], axis=1) + consts[...]
    row = lax.broadcasted_iota(jnp.int32, (8, rows), 0)
    stats = jnp.concatenate([jnp.where(row == 0, total, squares), blank[:8]], axis=1)
    rank = lax.axis_index("tp")
    for i, out in enumerate(outs):
        block = entry(routes[i], rank)
        for half in range(2):
            out[8 * half : 8 * half + 8] = scratch[pl.ds(pl.multiple_of((half * tp + block) * 8, 8), 8)]
        out[16:24] = stats


def total_kernel(crossing, own, *rest):
    arrived, (mine, other) = rest[:-2], rest[-2:]
    totals = [own[...], jnp.zeros(own.shape, F32)]
    for cross, block in zip(crossing, arrived):
        totals[cross] = totals[cross] + block[...]
    first = lax.axis_index("cfg") == 0
    for i, total in enumerate(totals):
        low, high, stats = total[0:8], total[8:16], total[16:24]
        at = 16 * i
        mine[at : at + 8] = jnp.where(first, low, high)
        other[at : at + 8] = jnp.where(first, high, low)
        mine[at + 8 : at + 16] = stats
        other[at + 8 : at + 16] = stats


def step_kernel(features, mine, theirs, coefs, out):
    rows = out.shape[1]
    consts = mine[0:8, rows : rows + 2] + mine[16:24, rows : rows + 2]

    def predict(block):
        sums = block[0:8, :rows]
        mean = block[8:9, :rows] / features
        square = block[9:10, :rows] / features
        spread = lax.rsqrt(square - mean * mean + final_eps)
        return spread * (sums - mean * consts[:, 0:1]) + consts[:, 1:2]

    own, partner = predict(mine[0:16] + theirs[16:32]), predict(mine[16:32] + theirs[0:16])
    is_conditioned = lax.axis_index("cfg") == 0
    conditioned = jnp.where(is_conditioned, own, partner)
    unconditioned = jnp.where(is_conditioned, partner, own)
    guided = unconditioned + guide_scale * (conditioned - unconditioned)
    root_now, rest_now, root_next, rest_next, live, latents = (
        coefs[8 * i : 8 * i + 8, :rows] for i in range(6)
    )
    clean = root_now * latents - rest_now * guided
    noise = root_now * guided + rest_now * latents
    out[...] = jnp.where(live > 0.0, root_next * clean + rest_next * noise, 0.0)


def exchange(value, axis, distance):
    return lax.ppermute(value, axis, [(i, i ^ distance) for i in range(lax.axis_size(axis))])


def send(value, route, cross=False):
    if not cross:
        return lax.ppermute(value, "tp", list(enumerate(route)))
    tp = len(route)
    pairs = [(half * tp + i, (1 - half) * tp + to) for half in range(2) for i, to in enumerate(route)]
    return lax.ppermute(value, ("cfg", "tp"), pairs)


def entry(route, rank):
    place = jnp.int32(route[0])
    for i, to in enumerate(route[1:], 1):
        place = jnp.where(rank == i, to, place)
    return place


def shards(
    stream, queries, keys, values, text_keys, text_values, out_weight, gate, shift, scale, proj_weight,
    q_gain, k_gain, lengths, latents, alphas, step_index,
):
    blocks = lax.axis_size("seq")
    tp = lax.axis_size("tp")
    rows, width = queries.shape[1:]
    columns = stream.shape[2]
    text = text_keys.shape[1]
    channels = proj_weight.shape[1]
    pairs = width // PAIR
    direct = blocks <= 4 and blocks & (blocks - 1) == 0
    q_gain, k_gain = q_gain.reshape(1, HEAD), k_gain.reshape(1, HEAD)
    one_gain = pltpu.VMEM(q_gain.shape, F32)
    counts = pltpu.SMEM(lengths.shape, jnp.int32)

    (packed,) = call(
        functools.partial(pack_keys_kernel, blocks),
        [vmem((rows, 2 * width), BF16)],
        "hhhh",
        [counts, pltpu.VMEM(keys.shape, BF16), pltpu.VMEM(values.shape, BF16), one_gain, pltpu.SemaphoreType.DMA((4,))],
        cost=2000000,
    )(lengths, keys, values, k_gain)
    if direct:
        gathered = [packed] + [exchange(packed, "seq", d) for d in range(blocks - 1, 0, -1)]
        order = lambda rank: [rank] + [rank ^ d for d in range(blocks - 1, 0, -1)]
    else:
        gathered = [lax.all_gather(packed, "seq", axis=0, tiled=True)]
        order = lambda rank: range(blocks)
    stacked, text_scores, bias, held_values, held_weight = call(
        functools.partial(queries_kernel, blocks, order),
        [
            vmem((pairs, 2 * rows, PAIR), BF16),
            vmem((pairs, 2 * rows, text)),
            vmem((1, blocks * rows)),
            vmem(text_values.shape, BF16),
            vmem(out_weight.shape, BF16),
        ],
        "hhhhhhh",
        [
            counts, pltpu.VMEM(queries.shape, BF16), pltpu.VMEM(text_keys.shape, BF16), one_gain, one_gain,
            pltpu.SemaphoreType.DMA((7,)),
        ],
        cost=20000000,
    )(lengths, queries, text_keys, q_gain, k_gain, text_values, out_weight)
    distances = range(tp - 1, 0, -1)
    routes = [[i ^ d for i in range(tp)] for d in distances]
    crossing = [CROSS[d % 2] for d in distances]
    attended, *outgoing = call(
        functools.partial(attend_kernel, len(gathered), lambda rank: [entry(r, rank) for r in routes]),
        [vmem((rows, width), BF16)] + [vmem((rows, columns), BF16)] * (tp - 1),
        "v" * (5 + len(gathered)),
        cost=100000000,
    )(stacked, text_scores, bias, held_values, held_weight, *gathered)
    arrived = [send(block, r) for r, block in zip(routes, outgoing)]
    base, factor, split, consts, coefs = call(
        functools.partial(residual_kernel, tp),
        [
            vmem((rows, columns)),
            vmem((rows, columns)),
            vmem((3 * channels + 16, columns), BF16),
            vmem((channels, LANES)),
            vmem((48, LANES)),
        ],
        "sss" + "v" * 8,
        cost=100000000,
    )(
        lengths, alphas, step_index, attended, held_weight, stream, gate.reshape(1, columns),
        shift.reshape(1, columns), scale.reshape(1, columns), proj_weight.T, latents.T,
    )
    hidden, *partials = call(
        functools.partial(hidden_kernel, tp, [list(range(tp))] + routes),
        [vmem((rows, columns), BF16)] + [vmem((24, LANES))] * tp,
        "v" * (4 + tp - 1),
        [pltpu.VMEM((channels, LANES), F32)],
        cost=20000000,
    )(base, factor, split, consts, *arrived)
    shares = [send(block, r, cross) for r, cross, block in zip(routes, crossing, partials[1:])]
    (hidden_out,) = call(
        keep_kernel, [(jax.ShapeDtypeStruct(stream.shape, BF16), "h")], "v", [pltpu.SemaphoreType.DMA((1,))], cost=2000000
    )(hidden)
    mine, other = call(functools.partial(total_kernel, crossing), [vmem((32, LANES))] * 2, "v" * tp)(partials[0], *shares)
    theirs = exchange(other, "cfg", 1)
    (latents_out,) = call(
        functools.partial(step_kernel, columns * tp), [vmem((latents.shape[1], rows))], "vvv"
    )(mine, theirs, coefs)
    return hidden_out, latents_out.T


def solution(mesh):
    return jax.shard_map(
        shards,
        mesh=mesh,
        in_specs=(
            P("cfg", "seq", "tp"),
            P("cfg", "seq", "tp"),
            P("cfg", "seq", "tp"),
            P("cfg", "seq", "tp"),
            P("cfg", None, "tp"),
            P("cfg", None, "tp"),
            P("tp", None),
            P("tp"),
            P("tp"),
            P("tp"),
            P("tp", None),
            P(),
            P(),
            P(),
            P("seq", ("cfg", "tp")),
            P(),
            P(),
        ),
        out_specs=(P("cfg", "seq", "tp"), P("seq", ("cfg", "tp"))),
        check_vma=False,
    )
```
